32 devices in a mesh: group: 2 (over x), expert: 4 (over y, core), dp: 4 (over z).
Axes of the slice: x: 2, y: 2, z: 4, core: 2. Of those that a mesh axis runs over, the one named last changes fastest.
Arguments:
- tokens: bfloat16 [4608, 7168], P(('group', 'expert', 'dp')), parts along dimension 0, may hold values from -4 to 4
- counts: int32 [32], P(('group', 'expert', 'dp')), parts along dimension 0, may hold values from 0 to 144, as said below
- send_counts: int32 [32, 4], P(('group', 'expert', 'dp')), parts along dimension 0, may hold values from 0 to 48, as said below
- routes: int32 [4608, 8], P(('group', 'expert', 'dp')), parts along dimension 0, may hold values from 0 to 255, as said below
- route_weights: bfloat16 [4608, 8], P(('group', 'expert', 'dp')), parts along dimension 0, may hold values from 0.099609375 to 0.59765625
- norm_gain: bfloat16 [7168], replicated, may hold values from 0.099609375 to 1.8984375
- w_gate: bfloat16 [4, 7168, 1024], P('expert', None, 'dp'), may hold values from -0.0625 to 0.0625
- w_up: bfloat16 [4, 7168, 1024], P('expert', None, 'dp'), may hold values from -0.0625 to 0.0625
- w_down: bfloat16 [4, 1024, 7168], P('expert', 'dp'), may hold values from -0.1875 to 0.1875
Outputs:
- mixed: bfloat16 [3072, 7168], P(('group', 'expert', 'dp')), parts along dimension 0
The draws below stay inside these ranges and needn't reach their ends.
There are 2 independent parts, one for each index of `group`. The reference program is written for one: setup_inputs(seed, part) draws one part's arguments, and reference() takes and returns one part's arrays. A program takes and returns all parts, laid end to end along the dimension named above; an argument that names none is the same for every part. Nothing has to cross between parts.
Inputs may be any that keep to these rules, and one draw needn't show every extreme that they name: `counts`: in every expert index some device holds 144 valid rows. send_counts[i, d] = 0 for d the dp index of device i, and a device hands at most counts[i] rows in all; after the moves every device holds at most 96 rows, and in every expert index some device holds exactly 96; in every expert index some entry is exactly 48. `routes`: the 8 ids of a row differ; experts 0 to 3 are held here, expert x on index x of expert, the others lie outside. Among the live rows a device holds after the rebalance, each expert held here is named by 1 to 4 rows, and one of them, the same on every device, by exactly 4 rows on every device.
All inputs are finite; a program needn't handle non-finite values.
Results may differ from the reference program's by a relative error of at most 0.0025.
Values may be sent and summed in bfloat16 or wider, within the bound.
A program may use at most 128 MiB of HBM per device.

```python
from functools import partial
import jax
import jax.numpy as jnp
from jax import lax

D = 7168
ROUTED = 256
TOP = 8
FF = 1024
BAL = 96
T_MAX = 48
CAP = 144
M = 4
EXPERTS = 4
ROWS_IN = 2304
N_EXPERT = 4
N_DP = 4


def rebalance_plan(key):
    plan_keys = jax.random.split(key, 3)
    group_ids = jnp.arange(N_EXPERT, dtype=jnp.int32)
    shuffled = jax.vmap(lambda subkey: jax.random.permutation(subkey, N_DP))(jax.random.split(plan_keys[0], N_EXPERT)).astype(jnp.int32)
    heavier = shuffled[:, 0::2]
    lighter = shuffled[:, 1::2]
    moving = jax.random.randint(plan_keys[1], (N_EXPERT, N_DP // 2), 0, T_MAX + 1, dtype=jnp.int32)
    moving = moving.at[:, 0].set(T_MAX)
    settled = jax.random.randint(plan_keys[2], (N_EXPERT, N_DP), BAL // 2, BAL + 1, dtype=jnp.int32)
    settled = settled.at[group_ids, heavier[:, 0]].set(BAL)
    holding = settled.at[group_ids[:, None], heavier].add(moving).at[group_ids[:, None], lighter].add(-moving)
    sending = jnp.zeros((N_EXPERT, N_DP, N_DP), jnp.int32).at[group_ids[:, None], heavier, lighter].set(moving)
    return (holding, sending, settled)


def draw_counts(key, part):
    holding, sending, settled = rebalance_plan(key)
    return holding.reshape(-1)


def draw_send_counts(key, part):
    holding, sending, settled = rebalance_plan(key)
    return sending.reshape(N_EXPERT * N_DP, N_DP)


def draw_routes(key, part):
    holding, sending, settled = rebalance_plan(key)
    key = jax.random.fold_in(key, 7)
    route_keys = jax.random.split(key, 6)
    devices = N_EXPERT * N_DP
    halves = EXPERTS // 2
    pairing = jax.vmap(lambda subkey: jax.random.permutation(subkey, EXPERTS))(jax.random.split(route_keys[0], devices)).astype(jnp.int32)
    first_of = pairing[:, 0::2]
    second_of = pairing[:, 1::2]
    load_count = jax.random.randint(route_keys[1], (devices, EXPERTS), 1, M + 1, dtype=jnp.int32)
    busiest = jax.random.randint(route_keys[2], (), 0, EXPERTS, dtype=jnp.int32)
    load_count = jnp.where(jnp.arange(EXPERTS, dtype=jnp.int32)[None, :] == busiest, M, load_count)
    live_rows = jnp.arange(BAL, dtype=jnp.int32)[None, :] < settled.reshape(devices, 1)
    scores = jax.random.randint(route_keys[3], (devices, halves, BAL), 0, 1 << 20, dtype=jnp.int32) + jnp.where(live_rows, 0, 1 << 21)[:, None, :]
    ordering = jnp.argsort(scores, axis=-1, stable=True)
    standing = jnp.argsort(ordering, axis=-1, stable=True).astype(jnp.int32)
    first_load = jnp.take_along_axis(load_count, first_of, axis=1)[:, :, None]
    second_load = jnp.take_along_axis(load_count, second_of, axis=1)[:, :, None]
    window_ids = jnp.where(standing < first_load, first_of[:, :, None], jnp.where(standing < first_load + second_load, second_of[:, :, None], -1))
    pool_size = (ROUTED - EXPERTS) // TOP
    outside = EXPERTS + jnp.arange(TOP, dtype=jnp.int32)[None, :, None] * pool_size + jax.random.randint(route_keys[4], (devices, TOP, BAL), 0, pool_size, dtype=jnp.int32)
    upper_part = jnp.where(window_ids >= 0, window_ids, outside[:, :halves, :])
    columns = jnp.swapaxes(jnp.concatenate([upper_part, outside[:, halves:, :]], axis=1), 1, 2)
    shuffle = jnp.argsort(jax.random.randint(route_keys[5], (devices, BAL, TOP), 0, 1 << 20, dtype=jnp.int32), axis=-1, stable=True)
    balanced = jnp.take_along_axis(columns, shuffle, axis=-1).reshape(devices * BAL, TOP).astype(jnp.int32)
    kept_rows = (holding - jnp.sum(sending, axis=2)).astype(jnp.int32)
    out_offset = (jnp.cumsum(sending, axis=2) - sending).astype(jnp.int32)
    arrivals = jnp.swapaxes(sending, 1, 2)
    in_offset = jnp.swapaxes(jnp.cumsum(arrivals, axis=2) - arrivals, 1, 2).astype(jnp.int32)
    slot_ids = jnp.arange(CAP, dtype=jnp.int32)
    beyond = slot_ids[None, None, :] - kept_rows[:, :, None]
    hit_table = (beyond[..., None] >= out_offset[:, :, None, :]) & (beyond[..., None] < (out_offset + sending)[:, :, None, :])
    dest_ids = jnp.arange(N_DP, dtype=jnp.int32)
    group_base = (jnp.arange(N_EXPERT, dtype=jnp.int32) * N_DP)[:, None, None, None]
    target = (group_base + dest_ids) * BAL + kept_rows[:, None, None, :] + in_offset[:, :, None, :] + beyond[..., None] - out_offset[:, :, None, :]
    moved_index = jnp.sum(jnp.where(hit_table, target, 0), axis=3)
    own_index = jnp.arange(devices, dtype=jnp.int32).reshape(N_EXPERT, N_DP, 1) * BAL + jnp.minimum(slot_ids, BAL - 1)[None, None, :]
    row_index = jnp.where(slot_ids[None, None, :] < kept_rows[:, :, None], own_index, jnp.where(jnp.any(hit_table, axis=3), moved_index, own_index))
    return balanced[row_index.reshape(-1).astype(jnp.int32)]


def block_scale(own_key, dims, cuts, least, high):
    def one(dim, shards_of):
        steps = jax.random.uniform(jax.random.fold_in(jax.random.fold_in(own_key, 6), dim), (shards_of,), jnp.float32, least / len(cuts), high / len(cuts))
        return jnp.repeat(jnp.exp(steps), dims[dim] // shards_of).reshape((-1,) + (1,) * (len(dims) - dim - 1))

    level = one(*cuts[0])
    for cut in cuts[1:]:
        level = level * one(*cut)
    return level


def scatter_about(own_key, dims, width, reach, shards=(), held_as=jnp.bfloat16):
    factor_of = block_scale(own_key, dims, shards, -0.22, 0.18) if shards else 1.0
    result = jax.random.normal(own_key, dims, jnp.float32) * width * factor_of
    return jnp.minimum(jnp.maximum(result, -reach), reach).astype(held_as)


def setup_inputs(seed: int = 0, part: int = 0) -> dict:
    key_list = jax.random.split(jax.random.key(seed), 10)
    part_splits = jax.random.split(jax.random.fold_in(key_list[9], part), 10)
    tokens = scatter_about(part_splits[0], (ROWS_IN, D), 1.0, 4.0, ((0, 16),))
    counts = draw_counts(jax.random.fold_in(jax.random.fold_in(key_list[9], part), 71), part)
    send_counts = draw_send_counts(jax.random.fold_in(jax.random.fold_in(key_list[9], part), 71), part)
    routes = draw_routes(jax.random.fold_in(jax.random.fold_in(key_list[9], part), 71), part)
    route_weights = jnp.clip(0.099609375 + 0.49804688 * jax.random.uniform(part_splits[4], (ROWS_IN, TOP), jnp.float32) ** block_scale(part_splits[4], (ROWS_IN, TOP), ((0, 16),), -0.2, 0.2), 0.099609375, 0.59765625).astype(jnp.bfloat16)
    norm_gain = jnp.clip(1.0 + 0.18 * jax.random.normal(key_list[5], (D,), jnp.float32), 0.099609375, 1.8984375).astype(jnp.bfloat16)
    w_gate = scatter_about(key_list[6], (EXPERTS, D, FF), D ** -0.5, 0.0625, ((0, 4), (2, 4)))
    w_up = scatter_about(key_list[7], (EXPERTS, D, FF), D ** -0.5, 0.0625, ((0, 4), (2, 4)))
    w_down = scatter_about(key_list[8], (EXPERTS, FF, D), FF ** -0.5, 0.1875, ((0, 4), (1, 4)))
    return {"tokens": tokens, "counts": counts, "send_counts": send_counts, "routes": routes, "route_weights": route_weights, "norm_gain": norm_gain, "w_gate": w_gate, "w_up": w_up, "w_down": w_down}


EPSILON = 1e-06

def rms_normed(row_block, norm_gain):
    values = row_block.astype(jnp.float32)
    scale_row = lax.rsqrt(lax.optimization_barrier(jnp.mean(values * values, axis=-1, keepdims=True)) + EPSILON)
    return (values * scale_row * norm_gain.astype(jnp.float32)).astype(jnp.bfloat16)

def slot_tables(routes_bal, live_rows, experts_here, capacity):
    expert_ids = jnp.arange(experts_here, dtype=jnp.int32)
    matches = (routes_bal[:, :, None] == expert_ids[None, None, :]) & live_rows[:, None, None]
    is_named = jnp.any(matches, axis=1)
    order_rank = (jnp.cumsum(is_named.astype(jnp.int32), axis=0) - 1).astype(jnp.int32)
    placed = (order_rank[:, :, None] == jnp.arange(capacity, dtype=jnp.int32)[None, None, :]) & is_named[:, :, None]
    return (matches, placed)

def combine_matrix(matches, placed, weights_bal):
    weight_each = lax.optimization_barrier(jnp.sum(weights_bal.astype(jnp.float32)[:, :, None] * matches, axis=1))
    weight_table = weight_each[:, :, None] * placed
    return weight_table.reshape(weight_table.shape[0], -1)

def rebalance_index(counts, send_counts):
    sending = send_counts.reshape(N_EXPERT, N_DP, N_DP)
    kept_rows = (counts.reshape(N_EXPERT, N_DP) - lax.optimization_barrier(jnp.sum(sending, axis=2))).astype(jnp.int32)
    out_offset = (jnp.cumsum(sending, axis=2) - sending).astype(jnp.int32)
    arrivals = jnp.swapaxes(sending, 1, 2).astype(jnp.int32)
    in_offset = (jnp.cumsum(arrivals, axis=2) - arrivals).astype(jnp.int32)
    position = jnp.arange(BAL, dtype=jnp.int32)
    own_rows = position[None, None, :] < kept_rows[:, :, None]
    beyond = position[None, None, :] - kept_rows[:, :, None]
    lower = in_offset[:, :, None, :]
    hit_table = (beyond[..., None] >= lower) & (beyond[..., None] < lower + arrivals[:, :, None, :])
    source_base = (jnp.arange(N_EXPERT, dtype=jnp.int32)[:, None] * N_DP + jnp.arange(N_DP, dtype=jnp.int32)[None, :]) * CAP
    source_row = source_base[:, None, None, :] + kept_rows[:, None, None, :] + jnp.swapaxes(out_offset, 1, 2)[:, :, None, :] + beyond[..., None] - lower
    moved_index = lax.optimization_barrier(jnp.sum(jnp.where(hit_table, source_row, 0), axis=3)).astype(jnp.int32)
    own_index = (source_base[:, :, None] + position[None, None, :]).astype(jnp.int32)
    row_index = jnp.where(own_rows, own_index, moved_index).astype(jnp.int32)
    live_rows = own_rows | jnp.any(hit_table, axis=3)
    return (row_index.reshape(-1), live_rows.reshape(-1))

def expert_pass(operands):
    row_block, gate_w, up_w, down_w = operands
    flat_rows = row_block.reshape(-1, D)
    gate_part = jnp.dot(flat_rows, gate_w, preferred_element_type=jnp.float32)
    upward = jnp.dot(flat_rows, up_w, preferred_element_type=jnp.float32)
    hidden = (jax.nn.silu(gate_part) * upward).astype(jnp.bfloat16)
    unit_width = FF // N_DP
    pieces = jnp.einsum('rkf,kfd->rkd', hidden.reshape(-1, N_DP, unit_width).astype(jnp.float32), down_w.reshape(N_DP, unit_width, D).astype(jnp.float32))
    rounded = lax.optimization_barrier(pieces.astype(jnp.bfloat16))
    output = lax.optimization_barrier(jnp.sum(rounded.astype(jnp.float32), axis=1)).astype(jnp.bfloat16)
    return output.reshape(row_block.shape)

def finish(operands):
    weight_table, outputs, row_block = operands
    mixed_in = jnp.dot(weight_table, outputs.astype(jnp.float32), precision=lax.Precision.HIGHEST)
    return (row_block.astype(jnp.float32) + mixed_in).astype(jnp.bfloat16)

def reference(tokens, counts, send_counts, routes, route_weights, norm_gain, w_gate, w_up, w_down):
    devices = N_EXPERT * N_DP
    row_index, live_rows = rebalance_index(counts, send_counts)
    zero_half = jnp.zeros((), jnp.bfloat16)
    moved_rows = jnp.where(live_rows[:, None], tokens[row_index], zero_half)
    routes_bal = routes[row_index].reshape(devices, BAL, TOP)
    weights_bal = route_weights[row_index].reshape(devices, BAL, TOP)
    live_dev = live_rows.reshape(devices, BAL)
    normed = rms_normed(moved_rows, norm_gain)
    matches, placed = jax.vmap(partial(slot_tables, experts_here=EXPERTS, capacity=M))(routes_bal, live_dev)
    position = jnp.arange(BAL, dtype=jnp.int32)
    slot_index = lax.optimization_barrier(jnp.sum(jnp.where(placed, position[None, :, None, None], 0), axis=1)).astype(jnp.int32)
    filled = jnp.any(placed, axis=1)
    row_base = (jnp.arange(devices, dtype=jnp.int32) * BAL)[:, None, None]
    slot_rows = jnp.where(filled[..., None], normed[(row_base + slot_index).astype(jnp.int32)], zero_half)
    by_expert = jnp.swapaxes(slot_rows, 0, 1)
    expert_out = lax.map(expert_pass, (by_expert, w_gate, w_up, w_down))
    per_device = jnp.swapaxes(expert_out, 0, 1).reshape(devices, EXPERTS * M, D)
    tables = jax.vmap(combine_matrix)(matches, placed, weights_bal)
    mixed_rows = lax.map(finish, (tables, per_device, moved_rows.reshape(devices, BAL, D)))
    return mixed_rows.reshape(devices * BAL, D)
```

```python
import functools
import jax
import jax.numpy as jnp
from jax import lax
from jax.experimental import pallas as pl
from jax.experimental.pallas import tpu as pltpu
from jax.sharding import PartitionSpec as P

BAL = 96
T_MAX = 48
M = 4
EPSILON = 1e-06
LANES = 128
CHUNK = 1024
MESH = pl.DeviceIdType.MESH
BF = jnp.bfloat16
F32 = jnp.float32


def dot(a, b):
    return jnp.dot(a.astype(BF), b.astype(BF), preferred_element_type=F32)


def dot_nt(a, b):
    return lax.dot_general(
        a.astype(BF), b.astype(BF), (((1,), (1,)), ((), ())), preferred_element_type=F32
    )


def iota(shape, dim):
    return lax.broadcasted_iota(jnp.int32, shape, dim).astype(F32)


def kernel(n_e, n_d, tokens, fields, plan, gain, wg_hbm, wu_hbm, wd_hbm, out,
           wg, wu, wd, meta_out, meta_in, rows_out, rest_out, rows_in, rest_in,
           acc, wide, send1, recv1, recv2, recv3, send4, recv4, gate, up,
           w_sem, meta_s, meta_r, rows_s, rows_r, rest_s, rest_r,
           s1, r1, s2, r2, s3, r3, s4, r4):
    e, d = lax.axis_index("expert"), lax.axis_index("dp")
    width = tokens.shape[1]
    cap = tokens.shape[0]
    slots = n_e * M
    first = rows_out.shape[1]
    rest = T_MAX - first
    chunks = width // CHUNK
    dps = [lax.rem(d + k, n_d) for k in range(1, n_d)]
    exs = [lax.rem(e + k, n_e) for k in range(1, n_e)]

    def each_chunk(fn):
        def step(c, carry):
            fn(pl.ds(pl.multiple_of(c * CHUNK, CHUNK), CHUNK))
            return carry
        lax.fori_loop(0, chunks, step, 0)

    def remote(src, dst, send, recv, device):
        return pltpu.make_async_remote_copy(
            src_ref=src, dst_ref=dst, send_sem=send, recv_sem=recv,
            device_id=device, device_id_type=MESH)

    loads = [pltpu.make_async_copy(a, b, w_sem.at[i])
             for i, (a, b) in enumerate(((wg_hbm, wg), (wu_hbm, wu), (wd_hbm, wd)))]
    for copy in loads:
        copy.start()

    barrier = pltpu.get_barrier_semaphore()
    for j in dps:
        pl.semaphore_signal(barrier, inc=1, device_id={"dp": j}, device_id_type=MESH)
    for x in exs:
        pl.semaphore_signal(barrier, inc=1, device_id={"expert": x}, device_id_type=MESH)

    lanes = plan.shape[1]
    upper = (iota((lanes, lanes), 0) < iota((lanes, lanes), 1)).astype(BF)
    target, named = plan[0:1, :], plan[1:2, :]
    picks = []
    for k, j in enumerate(dps):
        mine = (target == j.astype(F32)).astype(F32)
        ahead = mine * named
        behind = mine - ahead
        before_a = dot(jnp.broadcast_to(ahead, (8, lanes)), upper)[0:1]
        before_b = dot(jnp.broadcast_to(behind, (8, lanes)), upper)[0:1]
        total = jnp.sum(ahead, axis=1, keepdims=True)
        slot = jnp.where(ahead > 0, before_a, jnp.where(behind > 0, total + before_b, -1.0))
        pick = (iota((LANES, lanes), 0) == slot).astype(F32)
        meta_out[k] = dot_nt(fields[...], pick)
        picks.append(pick.astype(BF)[:T_MAX, :cap])

    pl.semaphore_wait(barrier, n_d - 1 + n_e - 1)
    meta_copies, row_copies, rest_copies = [], [], []
    for k, j in enumerate(dps):
        def pack(cols, k=k):
            block = dot(picks[k], tokens[:, cols]).astype(BF)
            rows_out[k, :, cols] = block[:first]
            if rest:
                rest_out[k, :, cols] = block[first:]
        copy = remote(meta_out.at[k], meta_in.at[d], meta_s.at[k], meta_r.at[d], {"dp": j})
        copy.start()
        meta_copies.append(copy)
        each_chunk(pack)
        copy = remote(rows_out.at[k], rows_in.at[d], rows_s.at[k], rows_r.at[d], {"dp": j})
        copy.start()
        row_copies.append(copy)

    def arrival(src, buf, sems, j, axis="dp"):
        return remote(src, buf.at[j], sems.at[j], sems.at[j], {axis: j})

    own = (target == -1.0).astype(F32)
    kept = jnp.sum(own, axis=1, keepdims=True)
    own_f = fields[...] * own
    rank_of = lax.broadcasted_iota(jnp.int32, (slots, 1), 0) % M
    rank_of = rank_of.astype(F32)
    base = jnp.zeros((slots, 1), F32)

    def place(weights, base, tri):
        has = (weights > 0).astype(F32)
        rank = dot(has, tri) + base
        placed = has * (rank == rank_of).astype(F32)
        return placed, base + jnp.sum(has, axis=1, keepdims=True)

    placed, base = place(own_f[:slots], base, upper)
    seat = jnp.where(own > 0, iota((1, lanes), 1), -1.0)
    a_own = (iota((BAL, lanes), 0) == seat).astype(F32)
    table = dot_nt(a_own, placed * own_f[:slots])
    a_own = a_own.astype(BF)[:, :cap]
    p_own = placed.astype(BF)[:, :cap]

    def own_part(cols):
        block = tokens[:, cols]
        acc[:, cols] = dot(a_own, block)
        wide[:, cols] = dot(p_own, block)
    each_chunk(own_part)

    meta_in[d] = jnp.zeros(meta_in.shape[1:], F32)
    for k, j in enumerate(dps):
        arrival(meta_out.at[k], meta_in, meta_r, j).wait_recv()
    tri = upper[:LANES, :LANES]
    offset = kept
    seats, places = [], []
    for j in range(n_d):
        f = meta_in[j]
        placed, base = place(f[:slots], base, tri)
        valid = f[slots:slots + 1]
        seat = jnp.where(valid > 0, f[slots + 1:slots + 2] + offset, -1.0)
        offset = offset + jnp.sum(valid, axis=1, keepdims=True)
        a = (iota((BAL, LANES), 0) == seat).astype(F32)
        table = table + dot_nt(a, placed * f[:slots])
        seats.append(a.astype(BF)[:, :T_MAX])
        places.append(placed.astype(BF)[:, :first])

    rows_in[d] = jnp.zeros(rows_in.shape[1:], BF)
    for k, j in enumerate(dps):
        arrival(rows_out.at[k], rows_in, rows_r, j).wait_recv()

    def named_part(cols):
        total = wide[:, cols]
        for j in range(n_d):
            total = total + dot(places[j], rows_in[j, :, cols])
        wide[:, cols] = total
    each_chunk(named_part)

    def squares(c, carry):
        v = wide[:, pl.ds(pl.multiple_of(c * CHUNK, CHUNK), CHUNK)]
        return carry + jnp.sum(v * v, axis=1, keepdims=True)
    scale = lax.rsqrt(lax.fori_loop(0, chunks, squares, jnp.zeros((slots, 1), F32)) / width + EPSILON)

    def norm(cols):
        wide[:, cols] = wide[:, cols] * scale * gain[:, cols]
        for x in range(n_e):
            send1[x, :, cols] = wide[x * M:(x + 1) * M, cols].astype(BF)
    each_chunk(norm)

    one_copies = []
    for k, x in enumerate(exs):
        copy = remote(send1.at[x], recv1.at[e], s1.at[k], r1.at[e], {"expert": x})
        copy.start()
        one_copies.append(copy)
    recv1[e] = send1[e]
    for k, x in enumerate(exs):
        arrival(send1.at[x], recv1, r1, x, "expert").wait_recv()

    def gather(cols):
        for x in range(n_e):
            wide[x * M:(x + 1) * M, cols] = recv1[x, :, cols].astype(F32)
        recv2[d, :, cols] = wide[:, cols].astype(BF)
    each_chunk(gather)

    two_copies = []
    for k, j in enumerate(dps):
        copy = remote(recv2.at[d], recv2.at[d], s2.at[k], r2.at[d], {"dp": j})
        copy.start()
        two_copies.append(copy)
    if rest:
        for k, j in enumerate(dps):
            copy = remote(rest_out.at[k], rest_in.at[d], rest_s.at[k], rest_r.at[d], {"dp": j})
            copy.start()
            rest_copies.append(copy)

    def got_part(cols):
        total = acc[:, cols]
        for j in range(n_d):
            total = total + dot(seats[j][:, :first], rows_in[j, :, cols])
        acc[:, cols] = total
    each_chunk(got_part)
    for copy in loads:
        copy.wait()
    for k, j in enumerate(dps):
        arrival(recv2.at[d], recv2, r2, j).wait_recv()

    gate[...] = jnp.zeros_like(gate)
    up[...] = jnp.zeros_like(up)

    def project(cols):
        x = recv2[:, :, cols].reshape(n_d * slots, CHUNK)
        gate[...] += dot(x, wg[cols, :])
        up[...] += dot(x, wu[cols, :])
    each_chunk(project)
    g = gate[...]
    hidden = (g / (1.0 + jnp.exp(-g)) * up[...]).astype(BF)
    for copy in two_copies:
        copy.wait_send()

    def down(cols):
        piece = dot(hidden, wd[:, cols]).astype(BF)
        recv2[:, :, cols] = piece.reshape(n_d, slots, CHUNK)
    each_chunk(down)
    three_copies = []
    for k, j in enumerate(dps):
        copy = remote(recv2.at[j], recv3.at[d], s3.at[k], r3.at[d], {"dp": j})
        copy.start()
        three_copies.append(copy)
    for k, j in enumerate(dps):
        arrival(recv2.at[j], recv3, r3, j).wait_recv()

    def reduce(cols):
        total = recv2[d, :, cols].astype(F32)
        for j in dps:
            total = total + recv3[j, :, cols].astype(F32)
        wide[:, cols] = total
        for x in range(n_e):
            send4[x, :, cols] = wide[x * M:(x + 1) * M, cols].astype(BF)
    each_chunk(reduce)

    four_copies = []
    for k, x in enumerate(exs):
        copy = remote(send4.at[x], recv4.at[e], s4.at[k], r4.at[e], {"expert": x})
        copy.start()
        four_copies.append(copy)
    recv4[e] = send4[e]

    if rest:
        rest_in[d] = jnp.zeros(rest_in.shape[1:], BF)
        for k, j in enumerate(dps):
            arrival(rest_out.at[k], rest_in, rest_r, j).wait_recv()

        def rest_part(cols):
            total = acc[:, cols]
            for j in range(n_d):
                total = total + dot(seats[j][:, first:], rest_in[j, :, cols])
            acc[:, cols] = total
        each_chunk(rest_part)
    for k, x in enumerate(exs):
        arrival(send4.at[x], recv4, r4, x, "expert").wait_recv()
    table = table.astype(BF)

    def finish(cols):
        for x in range(n_e):
            wide[x * M:(x + 1) * M, cols] = recv4[x, :, cols].astype(F32)
        out[:, cols] = (acc[:, cols] + dot(table, wide[:, cols])).astype(BF)
    each_chunk(finish)
    for copy in meta_copies + row_copies + rest_copies + one_copies + three_copies + four_copies:
        copy.wait_send()


def body(tokens, counts, send_counts, routes, route_weights, norm_gain, w_gate, w_up, w_down):
    n_e, n_d = lax.axis_size("expert"), lax.axis_size("dp")
    cap, width = tokens.shape
    part = w_gate.shape[2]
    slots = n_e * M
    first = min(T_MAX, slots)
    rest = T_MAX - first
    lanes = -(-cap // LANES) * LANES
    pad = ((0, 0), (0, lanes - cap))
    ids = jnp.pad(routes.T, pad, constant_values=-1)
    weights = jnp.pad(route_weights.T.astype(F32), pad)
    place = jnp.arange(lanes, dtype=jnp.int32)
    send_row = send_counts[0]
    begin = counts[0] - jnp.sum(send_row)
    target = jnp.where(place < begin, -1, -2)
    index = place
    for j in range(n_d):
        inside = (place >= begin) & (place < begin + send_row[j])
        target = jnp.where(inside, j, target)
        index = jnp.where(inside, place - begin, index)
        begin = begin + send_row[j]
    valid = (target > -2).astype(F32)
    chosen = jnp.stack(
        [jnp.sum(jnp.where(ids == x, weights, 0.0), axis=0) for x in range(n_e)]) * valid
    named = jnp.any(chosen > 0, axis=0).astype(F32)
    height = -(-(slots + 2) // 8) * 8
    fields = jnp.concatenate([
        jnp.repeat(chosen, M, axis=0), valid[None], index.astype(F32)[None],
        jnp.zeros((height - slots - 2, lanes), F32)])
    plan = jnp.concatenate([target.astype(F32)[None], named[None], jnp.zeros((6, lanes), F32)])
    gain = norm_gain.astype(F32)[None]

    vmem = pl.BlockSpec(memory_space=pltpu.VMEM)
    hbm = pl.BlockSpec(memory_space=pl.ANY)
    dma = pltpu.SemaphoreType.DMA
    return pl.pallas_call(
        functools.partial(kernel, n_e, n_d),
        out_shape=jax.ShapeDtypeStruct((BAL, width), BF),
        in_specs=[vmem] * 4 + [hbm] * 3,
        out_specs=vmem,
        scratch_shapes=[
            pltpu.VMEM((width, part), BF),
            pltpu.VMEM((width, part), BF),
            pltpu.VMEM((part, width), BF),
            pltpu.VMEM((n_d - 1, height, LANES), F32),
            pltpu.VMEM((n_d, height, LANES), F32),
            pltpu.VMEM((n_d - 1, first, width), BF),
            pltpu.VMEM((n_d - 1, max(rest, 16), width if rest else LANES), BF),
            pltpu.VMEM((n_d, first, width), BF),
            pltpu.VMEM((n_d, max(rest, 16), width if rest else LANES), BF),
            pltpu.VMEM((BAL, width), F32),
            pltpu.VMEM((slots, width), F32),
            pltpu.VMEM((n_e, M, width), BF),
            pltpu.VMEM((n_e, M, width), BF),
            pltpu.VMEM((n_d, slots, width), BF),
            pltpu.VMEM((n_d, slots, width), BF),
            pltpu.VMEM((n_e, M, width), BF),
            pltpu.VMEM((n_e, M, width), BF),
            pltpu.VMEM((n_d * slots, part), F32),
            pltpu.VMEM((n_d * slots, part), F32),
            dma((3,)),
            dma((n_d,)), dma((n_d,)),
            dma((n_d,)), dma((n_d,)),
            dma((n_d,)), dma((n_d,)),
            dma((n_e,)), dma((n_e,)),
            dma((n_d,)), dma((n_d,)),
            dma((n_d,)), dma((n_d,)),
            dma((n_e,)), dma((n_e,)),
        ],
        compiler_params=pltpu.CompilerParams(
            collective_id=0, has_side_effects=True, vmem_limit_bytes=60 * 1024 * 1024),
    )(tokens, fields, plan, gain, w_gate[0], w_up[0], w_down[0])


def solution(mesh):
    rows = P(("group", "expert", "dp"), None)
    in_specs = (
        rows,
        P(("group", "expert", "dp")),
        rows,
        rows,
        rows,
        P(),
        P("expert", None, "dp"),
        P("expert", None, "dp"),
        P("expert", "dp", None),
    )
    return jax.shard_map(body, mesh=mesh, in_specs=in_specs, out_specs=rows, check_vma=False)
```

```python
import functools
import jax
import jax.numpy as jnp
from jax import lax
from jax.experimental import pallas as pl
from jax.experimental.pallas import tpu as pltpu
from jax.sharding import PartitionSpec as P

BAL = 96
T_MAX = 48
M = 4
EPSILON = 1e-06
LANES = 128
CHUNK = 1024
MESH = pl.DeviceIdType.MESH
BF = jnp.bfloat16
F32 = jnp.float32


def dot(a, b):
    return jnp.dot(a.astype(BF), b.astype(BF), preferred_element_type=F32)


def dot_nt(a, b):
    return lax.dot_general(
        a.astype(BF), b.astype(BF), (((1,), (1,)), ((), ())), preferred_element_type=F32
    )


def iota(shape, dim):
    return lax.broadcasted_iota(jnp.int32, shape, dim).astype(F32)


def kernel(n_e, n_d, tokens, fields, plan, gain, wg_hbm, wu_hbm, wd_hbm, out,
           wg, wu, wd, meta_out, meta_in, rows_out, rest_out, rows_in, rest_in,
           acc, wide, send1, recv1, recv2, recv3, part_in, part_out, send4, recv4, gate, up,
           w_sem, meta_s, meta_r, rows_s, rows_r, rest_s, rest_r,
           s1, r1, s2, r2, s3, r3, sp, rp, s4, r4):
    e, d = lax.axis_index("expert"), lax.axis_index("dp")
    width = tokens.shape[1]
    cap = tokens.shape[0]
    slots = n_e * M
    first = rows_out.shape[1]
    rest = T_MAX - first
    chunks = width // CHUNK
    dps = [lax.rem(d + k, n_d) for k in range(1, n_d)]
    exs = [lax.rem(e + k, n_e) for k in range(1, n_e)]
    half = n_d // 2
    seat_of = lax.rem(d, half)
    near_seats = [lax.rem(seat_of + k, half) for k in range(1, half)]
    near = [d - seat_of + p for p in near_seats]
    partner = lax.rem(d + half, n_d)

    def each_chunk(fn):
        def step(c, carry):
            fn(pl.ds(pl.multiple_of(c * CHUNK, CHUNK), CHUNK))
            return carry
        lax.fori_loop(0, chunks, step, 0)

    def remote(src, dst, send, recv, device):
        return pltpu.make_async_remote_copy(
            src_ref=src, dst_ref=dst, send_sem=send, recv_sem=recv,
            device_id=device, device_id_type=MESH)

    loads = [pltpu.make_async_copy(a, b, w_sem.at[i])
             for i, (a, b) in enumerate(((wg_hbm, wg), (wu_hbm, wu), (wd_hbm, wd)))]
    for copy in loads:
        copy.start()

    barrier = pltpu.get_barrier_semaphore()
    for j in dps:
        pl.semaphore_signal(barrier, inc=1, device_id={"dp": j}, device_id_type=MESH)
    for x in exs:
        pl.semaphore_signal(barrier, inc=1, device_id={"expert": x}, device_id_type=MESH)

    lanes = plan.shape[1]
    upper = (iota((lanes, lanes), 0) < iota((lanes, lanes), 1)).astype(BF)
    target, named = plan[0:1, :], plan[1:2, :]
    picks = []
    for k, j in enumerate(dps):
        mine = (target == j.astype(F32)).astype(F32)
        ahead = mine * named
        behind = mine - ahead
        before_a = dot(jnp.broadcast_to(ahead, (8, lanes)), upper)[0:1]
        before_b = dot(jnp.broadcast_to(behind, (8, lanes)), upper)[0:1]
        total = jnp.sum(ahead, axis=1, keepdims=True)
        slot = jnp.where(ahead > 0, before_a, jnp.where(behind > 0, total + before_b, -1.0))
        pick = (iota((LANES, lanes), 0) == slot).astype(F32)
        meta_out[k] = dot_nt(fields[...], pick)
        picks.append(pick.astype(BF)[:T_MAX, :cap])

    pl.semaphore_wait(barrier, n_d - 1 + n_e - 1)
    meta_copies, row_copies, rest_copies = [], [], []
    for k, j in enumerate(dps):
        copy = remote(meta_out.at[k], meta_in.at[d], meta_s.at[k], meta_r.at[d], {"dp": j})
        copy.start()
        meta_copies.append(copy)
    head = jnp.concatenate([p[:first] for p in picks])

    def pack(cols):
        rows_out[:, :, cols] = dot(head, tokens[:, cols]).astype(BF).reshape(n_d - 1, first, CHUNK)
    each_chunk(pack)
    for k, j in enumerate(dps):
        copy = remote(rows_out.at[k], rows_in.at[d], rows_s.at[k], rows_r.at[d], {"dp": j})
        copy.start()
        row_copies.append(copy)
    if rest:
        tail = jnp.concatenate([p[first:] for p in picks])

        def pack_rest(cols):
            rest_out[:, :, cols] = dot(tail, tokens[:, cols]).astype(BF).reshape(n_d - 1, rest, CHUNK)
        each_chunk(pack_rest)
    batch = 16

    def rest_copy(k, j, slot, b):
        rows = pl.ds(b * batch, batch)
        return remote(rest_out.at[k, rows], rest_in.at[slot, rows],
                      rest_s.at[b, k], rest_r.at[b, slot], {"dp": j})

    def send_rest(b):
        if b * batch < rest:
            for k, j in enumerate(dps):
                copy = rest_copy(k, j, d, b)
                copy.start()
                rest_copies.append(copy)

    def arrival(src, buf, sems, j, axis="dp"):
        return remote(src, buf.at[j], sems.at[j], sems.at[j], {axis: j})

    own = (target == -1.0).astype(F32)
    kept = jnp.sum(own, axis=1, keepdims=True)
    own_f = fields[...] * own
    rank_of = lax.broadcasted_iota(jnp.int32, (slots, 1), 0) % M
    rank_of = rank_of.astype(F32)
    base = jnp.zeros((slots, 1), F32)

    def place(weights, base, tri):
        has = (weights > 0).astype(F32)
        rank = dot(has, tri) + base
        placed = has * (rank == rank_of).astype(F32)
        return placed, base + jnp.sum(has, axis=1, keepdims=True)

    placed, base = place(own_f[:slots], base, upper)
    seat = jnp.where(own > 0, iota((1, lanes), 1), -1.0)
    a_own = (iota((BAL, lanes), 0) == seat).astype(F32)
    table = dot_nt(a_own, placed * own_f[:slots])
    a_own = a_own.astype(BF)[:, :cap]
    p_own = placed.astype(BF)[:, :cap]

    def own_part(cols):
        block = tokens[:, cols]
        acc[:, cols] = dot(a_own, block)
        wide[:, cols] = dot(p_own, block)
    each_chunk(own_part)

    meta_in[d] = jnp.zeros(meta_in.shape[1:], F32)
    for k, j in enumerate(dps):
        arrival(meta_out.at[k], meta_in, meta_r, j).wait_recv()
    tri = upper[:LANES, :LANES]
    offset = kept
    seats, places = [], []
    for j in range(n_d):
        f = meta_in[j]
        placed, base = place(f[:slots], base, tri)
        valid = f[slots:slots + 1]
        seat = jnp.where(valid > 0, f[slots + 1:slots + 2] + offset, -1.0)
        offset = offset + jnp.sum(valid, axis=1, keepdims=True)
        a = (iota((BAL, LANES), 0) == seat).astype(F32)
        table = table + dot_nt(a, placed * f[:slots])
        seats.append(a.astype(BF)[:, :T_MAX])
        places.append(placed.astype(BF)[:, :first])

    rows_in[d] = jnp.zeros(rows_in.shape[1:], BF)
    for k, j in enumerate(dps):
        arrival(rows_out.at[k], rows_in, rows_r, j).wait_recv()
    send_rest(0)

    def named_part(cols):
        total = wide[:, cols]
        for j in range(n_d):
            total = total + dot(places[j], rows_in[j, :, cols])
        wide[:, cols] = total
    each_chunk(named_part)

    def squares(c, carry):
        v = wide[:, pl.ds(pl.multiple_of(c * CHUNK, CHUNK), CHUNK)]
        return carry + jnp.sum(v * v, axis=1, keepdims=True)
    scale = lax.rsqrt(lax.fori_loop(0, chunks, squares, jnp.zeros((slots, 1), F32)) / width + EPSILON)

    def norm(cols):
        wide[:, cols] = wide[:, cols] * scale * gain[:, cols]
        for x in range(n_e):
            send1[x, :, cols] = wide[x * M:(x + 1) * M, cols].astype(BF)
    each_chunk(norm)

    one_copies = []
    for k, x in enumerate(exs):
        copy = remote(send1.at[x], recv1.at[e], s1.at[k], r1.at[e], {"expert": x})
        copy.start()
        one_copies.append(copy)
    recv1[e] = send1[e]
    for k, x in enumerate(exs):
        arrival(send1.at[x], recv1, r1, x, "expert").wait_recv()

    def gather(cols):
        for x in range(n_e):
            wide[x * M:(x + 1) * M, cols] = recv1[x, :, cols].astype(F32)
        recv2[d, :, cols] = wide[:, cols].astype(BF)
    each_chunk(gather)

    two_copies = []
    copy = remote(recv2.at[d], recv2.at[d], s2.at[0], r2.at[d], {"dp": partner})
    copy.start()
    two_copies.append(copy)
    for k, j in enumerate(near):
        copy = remote(recv2.at[d], recv2.at[d], s2.at[1 + k], r2.at[d], {"dp": j})
        copy.start()
        two_copies.append(copy)
    arrival(recv2.at[d], recv2, r2, partner).wait_recv()
    for k, j in enumerate(near):
        copy = remote(recv2.at[partner], recv2.at[partner], s2.at[half + k], r2.at[partner], {"dp": j})
        copy.start()
        two_copies.append(copy)

    def got_part(cols):
        total = acc[:, cols]
        for j in range(n_d):
            total = total + dot(seats[j][:, :first], rows_in[j, :, cols])
        acc[:, cols] = total
    each_chunk(got_part)
    for copy in loads:
        copy.wait()
    for j in near:
        arrival(recv2.at[d], recv2, r2, j).wait_recv()
        arrival(recv2.at[d], recv2, r2, lax.rem(j + half, n_d)).wait_recv()
    send_rest(1)

    gate[...] = jnp.zeros_like(gate)
    up[...] = jnp.zeros_like(up)

    def project(cols):
        x = recv2[:, :, cols].reshape(n_d * slots, CHUNK)
        gate[...] += dot(x, wg[cols, :])
        up[...] += dot(x, wu[cols, :])
    each_chunk(project)
    g = gate[...]
    hidden = (g / (1.0 + jnp.exp(-g)) * up[...]).astype(BF)
    for copy in two_copies:
        copy.wait_send()

    def down(cols):
        piece = dot(hidden, wd[:, cols]).astype(BF)
        recv2[:, :, cols] = piece.reshape(n_d, slots, CHUNK)
    each_chunk(down)
    three_copies = []
    for k, (j, p) in enumerate(zip(near, near_seats)):
        copy = remote(recv2.at[lax.rem(j + half, n_d)], part_in.at[seat_of],
                      sp.at[k], rp.at[seat_of], {"dp": j})
        copy.start()
        three_copies.append(copy)
    for k, (j, p) in enumerate(zip(near, near_seats)):
        copy = remote(recv2.at[j], recv3.at[seat_of], s3.at[k], r3.at[seat_of], {"dp": j})
        copy.start()
        three_copies.append(copy)
    for p, j in zip(near_seats, near):
        remote(recv2.at[j], part_in.at[p], sp.at[0], rp.at[p], {"dp": j}).wait_recv()

    def partial_sum(cols):
        total = recv2[partner, :, cols].astype(F32)
        for p in near_seats:
            total = total + part_in[p, :, cols].astype(F32)
        part_out[:, cols] = total.astype(BF)
    each_chunk(partial_sum)
    copy = remote(part_out, recv3.at[half], s3.at[half - 1], r3.at[half], {"dp": partner})
    copy.start()
    three_copies.append(copy)
    for p, j in zip(near_seats, near):
        remote(recv2.at[j], recv3.at[p], s3.at[0], r3.at[p], {"dp": j}).wait_recv()
    copy.wait_recv()

    def reduce(cols):
        total = recv2[d, :, cols].astype(F32) + recv3[half, :, cols].astype(F32)
        for p in near_seats:
            total = total + recv3[p, :, cols].astype(F32)
        wide[:, cols] = total
        for x in range(n_e):
            send4[x, :, cols] = wide[x * M:(x + 1) * M, cols].astype(BF)
    each_chunk(reduce)

    four_copies = []
    for k, x in enumerate(exs):
        copy = remote(send4.at[x], recv4.at[e], s4.at[k], r4.at[e], {"expert": x})
        copy.start()
        four_copies.append(copy)
    recv4[e] = send4[e]

    if rest:
        rest_in[d] = jnp.zeros(rest_in.shape[1:], BF)
        for b in range(rest // batch):
            for k, j in enumerate(dps):
                rest_copy(k, j, j, b).wait_recv()

        def rest_part(cols):
            total = acc[:, cols]
            for j in range(n_d):
                total = total + dot(seats[j][:, first:], rest_in[j, :, cols])
            acc[:, cols] = total
        each_chunk(rest_part)
    for k, x in enumerate(exs):
        arrival(send4.at[x], recv4, r4, x, "expert").wait_recv()
    table = table.astype(BF)

    def finish(cols):
        for x in range(n_e):
            wide[x * M:(x + 1) * M, cols] = recv4[x, :, cols].astype(F32)
        out[:, cols] = (acc[:, cols] + dot(table, wide[:, cols])).astype(BF)
    each_chunk(finish)
    for copy in meta_copies + row_copies + rest_copies + one_copies + three_copies + four_copies:
        copy.wait_send()


def body(tokens, counts, send_counts, routes, route_weights, norm_gain, w_gate, w_up, w_down):
    n_e, n_d = lax.axis_size("expert"), lax.axis_size("dp")
    cap, width = tokens.shape
    part = w_gate.shape[2]
    slots = n_e * M
    first = min(T_MAX, slots)
    rest = T_MAX - first
    lanes = -(-cap // LANES) * LANES
    pad = ((0, 0), (0, lanes - cap))
    ids = jnp.pad(routes.T, pad, constant_values=-1)
    weights = jnp.pad(route_weights.T.astype(F32), pad)
    place = jnp.arange(lanes, dtype=jnp.int32)
    send_row = send_counts[0]
    begin = counts[0] - jnp.sum(send_row)
    target = jnp.where(place < begin, -1, -2)
    index = place
    for j in range(n_d):
        inside = (place >= begin) & (place < begin + send_row[j])
        target = jnp.where(inside, j, target)
        index = jnp.where(inside, place - begin, index)
        begin = begin + send_row[j]
    valid = (target > -2).astype(F32)
    chosen = jnp.stack(
        [jnp.sum(jnp.where(ids == x, weights, 0.0), axis=0) for x in range(n_e)]) * valid
    named = jnp.any(chosen > 0, axis=0).astype(F32)
    height = -(-(slots + 2) // 8) * 8
    fields = jnp.concatenate([
        jnp.repeat(chosen, M, axis=0), valid[None], index.astype(F32)[None],
        jnp.zeros((height - slots - 2, lanes), F32)])
    plan = jnp.concatenate([target.astype(F32)[None], named[None], jnp.zeros((6, lanes), F32)])
    gain = norm_gain.astype(F32)[None]

    vmem = pl.BlockSpec(memory_space=pltpu.VMEM)
    hbm = pl.BlockSpec(memory_space=pl.ANY)
    dma = pltpu.SemaphoreType.DMA
    return pl.pallas_call(
        functools.partial(kernel, n_e, n_d),
        out_shape=jax.ShapeDtypeStruct((BAL, width), BF),
        in_specs=[vmem] * 4 + [hbm] * 3,
        out_specs=vmem,
        scratch_shapes=[
            pltpu.VMEM((width, part), BF),
            pltpu.VMEM((width, part), BF),
            pltpu.VMEM((part, width), BF),
            pltpu.VMEM((n_d - 1, height, LANES), F32),
            pltpu.VMEM((n_d, height, LANES), F32),
            pltpu.VMEM((n_d - 1, first, width), BF),
            pltpu.VMEM((n_d - 1, max(rest, 16), width if rest else LANES), BF),
            pltpu.VMEM((n_d, first, width), BF),
            pltpu.VMEM((n_d, max(rest, 16), width if rest else LANES), BF),
            pltpu.VMEM((BAL, width), F32),
            pltpu.VMEM((slots, width), F32),
            pltpu.VMEM((n_e, M, width), BF),
            pltpu.VMEM((n_e, M, width), BF),
            pltpu.VMEM((n_d, slots, width), BF),
            pltpu.VMEM((n_d // 2 + 1, slots, width), BF),
            pltpu.VMEM((n_d // 2, slots, width), BF),
            pltpu.VMEM((slots, width), BF),
            pltpu.VMEM((n_e, M, width), BF),
            pltpu.VMEM((n_e, M, width), BF),
            pltpu.VMEM((n_d * slots, part), F32),
            pltpu.VMEM((n_d * slots, part), F32),
            dma((3,)),
            dma((n_d,)), dma((n_d,)),
            dma((n_d,)), dma((n_d,)),
            dma((2, n_d)), dma((2, n_d)),
            dma((n_e,)), dma((n_e,)),
            dma((n_d,)), dma((n_d,)),
            dma((n_d,)), dma((n_d,)),
            dma((n_d,)), dma((n_d,)),
            dma((n_e,)), dma((n_e,)),
        ],
        compiler_params=pltpu.CompilerParams(
            collective_id=0, has_side_effects=True, vmem_limit_bytes=60 * 1024 * 1024),
    )(tokens, fields, plan, gain, w_gate[0], w_up[0], w_down[0])


def solution(mesh):
    rows = P(("group", "expert", "dp"), None)
    in_specs = (
        rows,
        P(("group", "expert", "dp")),
        rows,
        rows,
        rows,
        P(),
        P("expert", None, "dp"),
        P("expert", None, "dp"),
        P("expert", "dp", None),
    )
    return jax.shard_map(body, mesh=mesh, in_specs=in_specs, out_specs=rows, check_vma=False)
```

```python
import functools
import jax
import jax.numpy as jnp
from jax import lax
from jax.experimental import pallas as pl
from jax.experimental.pallas import tpu as pltpu
from jax.sharding import PartitionSpec as P

BAL = 96
T_MAX = 48
M = 4
EPSILON = 1e-06
LANES = 128
CHUNK = 1024
MESH = pl.DeviceIdType.MESH
BF = jnp.bfloat16
F32 = jnp.float32


def dot(a, b):
    return jnp.dot(a.astype(BF), b.astype(BF), preferred_element_type=F32)


def dot_nt(a, b):
    return lax.dot_general(
        a.astype(BF), b.astype(BF), (((1,), (1,)), ((), ())), preferred_element_type=F32
    )


def iota(shape, dim):
    return lax.broadcasted_iota(jnp.int32, shape, dim).astype(F32)


def kernel(n_e, n_d, counts, send_counts, tokens, routes, weights, gain, wg_hbm, wu_hbm, wd_hbm, out,
           wg, wu, wd, meta_out, meta_in, rows_out, rest_out, rows_in, rest_in,
           acc, wide, send1, recv1, recv2, recv3, part_in, part_out, send4, recv4, gate, up,
           w_sem, meta_s, meta_r, rows_s, rows_r, rest_s, rest_r,
           s1, r1, s2, r2, s3, r3, sp, rp, s4, r4):
    e, d = lax.axis_index("expert"), lax.axis_index("dp")
    width = tokens.shape[1]
    cap = tokens.shape[0]
    slots = n_e * M
    first = rows_out.shape[1]
    rest = T_MAX - first
    chunks = width // CHUNK
    dps = [lax.rem(d + k, n_d) for k in range(1, n_d)]
    exs = [lax.rem(e + k, n_e) for k in range(1, n_e)]
    half = n_d // 2
    seat_of = lax.rem(d, half)
    near_seats = [lax.rem(seat_of + k, half) for k in range(1, half)]
    near = [d - seat_of + p for p in near_seats]
    partner = lax.rem(d + half, n_d)

    def each_chunk(fn):
        def step(c, carry):
            fn(pl.ds(pl.multiple_of(c * CHUNK, CHUNK), CHUNK))
            return carry
        lax.fori_loop(0, chunks, step, 0)

    def remote(src, dst, send, recv, device):
        return pltpu.make_async_remote_copy(
            src_ref=src, dst_ref=dst, send_sem=send, recv_sem=recv,
            device_id=device, device_id_type=MESH)

    loads = [pltpu.make_async_copy(a, b, w_sem.at[i])
             for i, (a, b) in enumerate(((wg_hbm, wg), (wu_hbm, wu), (wd_hbm, wd)))]
    for copy in loads:
        copy.start()

    barrier = pltpu.get_barrier_semaphore()
    for j in dps:
        pl.semaphore_signal(barrier, inc=1, device_id={"dp": j}, device_id_type=MESH)
    for x in exs:
        pl.semaphore_signal(barrier, inc=1, device_id={"expert": x}, device_id_type=MESH)

    lanes = -(-cap // LANES) * LANES
    ids, values = routes[...], weights[...].astype(F32)
    expert_of = lax.broadcasted_iota(jnp.int32, (1, LANES), 1) // M
    chosen = jnp.zeros((cap, LANES), F32)
    for x in range(n_e):
        column = jnp.sum(jnp.where(ids == x, values, 0.0), axis=1, keepdims=True)
        chosen = chosen + column * (expert_of == x).astype(F32)
    chosen = jnp.concatenate([chosen, jnp.zeros((lanes - cap, LANES), F32)])
    place_ids = lax.broadcasted_iota(jnp.int32, (1, lanes), 1)
    begin = counts[0]
    for j in range(n_d):
        begin = begin - send_counts[0, j]
    target = jnp.where(place_ids < begin, -1, -2)
    index = place_ids
    for j in range(n_d):
        after = begin + send_counts[0, j]
        inside = (place_ids >= begin) & (place_ids < after)
        target = jnp.where(inside, j, target)
        index = jnp.where(inside, place_ids - begin, index)
        begin = after
    target = target.astype(F32)
    valid = (target > -2.0).astype(F32)
    eye = (iota((slots, LANES), 0) == iota((slots, LANES), 1)).astype(F32)
    chosen = dot_nt(eye, chosen) * valid
    named = (jnp.max(chosen, axis=0, keepdims=True) > 0).astype(F32)
    low = iota((8, lanes), 0)
    fields = jnp.concatenate([
        chosen, jnp.where(low == 0, valid, jnp.where(low == 1, index.astype(F32), 0.0))])
    upper = (iota((lanes, lanes), 0) < iota((lanes, lanes), 1)).astype(BF)
    picks = []
    for k, j in enumerate(dps):
        mine = (target == j.astype(F32)).astype(F32)
        ahead = mine * named
        behind = mine - ahead
        before_a = dot(jnp.broadcast_to(ahead, (8, lanes)), upper)[0:1]
        before_b = dot(jnp.broadcast_to(behind, (8, lanes)), upper)[0:1]
        total = jnp.sum(ahead, axis=1, keepdims=True)
        slot = jnp.where(ahead > 0, before_a, jnp.where(behind > 0, total + before_b, -1.0))
        pick = (iota((LANES, lanes), 0) == slot).astype(F32)
        meta_out[k] = dot_nt(fields, pick)
        picks.append(pick.astype(BF)[:T_MAX, :cap])

    pl.semaphore_wait(barrier, n_d - 1 + n_e - 1)
    meta_copies, row_copies, rest_copies = [], [], []
    for k, j in enumerate(dps):
        copy = remote(meta_out.at[k], meta_in.at[d], meta_s.at[k], meta_r.at[d], {"dp": j})
        copy.start()
        meta_copies.append(copy)
    head = jnp.concatenate([p[:first] for p in picks])

    def pack(cols):
        rows_out[:, :, cols] = dot(head, tokens[:, cols]).astype(BF).reshape(n_d - 1, first, CHUNK)
    each_chunk(pack)
    for k, j in enumerate(dps):
        copy = remote(rows_out.at[k], rows_in.at[d], rows_s.at[k], rows_r.at[d], {"dp": j})
        copy.start()
        row_copies.append(copy)
    if rest:
        tail = jnp.concatenate([p[first:] for p in picks])

        def pack_rest(cols):
            rest_out[:, :, cols] = dot(tail, tokens[:, cols]).astype(BF).reshape(n_d - 1, rest, CHUNK)
        each_chunk(pack_rest)
    batch = 16

    def rest_copy(k, j, slot, b):
        rows = pl.ds(b * batch, batch)
        return remote(rest_out.at[k, rows], rest_in.at[slot, rows],
                      rest_s.at[b, k], rest_r.at[b, slot], {"dp": j})

    across = [lax.rem(j + half, n_d) for j in near]

    def send_rest(b, peers):
        if b * batch < rest:
            for j in peers:
                k = lax.rem(j - d - 1 + 2 * n_d, n_d)
                copy = rest_copy(k, j, d, b)
                copy.start()
                rest_copies.append(copy)

    def arrival(src, buf, sems, j, axis="dp"):
        return remote(src, buf.at[j], sems.at[j], sems.at[j], {axis: j})

    own = (target == -1.0).astype(F32)
    kept = jnp.sum(own, axis=1, keepdims=True)
    own_f = fields * own
    rank_of = lax.broadcasted_iota(jnp.int32, (slots, 1), 0) % M
    rank_of = rank_of.astype(F32)
    base = jnp.zeros((slots, 1), F32)

    def place(weights, base, tri):
        has = (weights > 0).astype(F32)
        rank = dot(has, tri) + base
        placed = has * (rank == rank_of).astype(F32)
        return placed, base + jnp.sum(has, axis=1, keepdims=True)

    placed, base = place(own_f[:slots], base, upper)
    seat = jnp.where(own > 0, iota((1, lanes), 1), -1.0)
    a_own = (iota((BAL, lanes), 0) == seat).astype(F32)
    table = dot_nt(a_own, placed * own_f[:slots])
    a_own = a_own.astype(BF)[:, :cap]
    p_own = placed.astype(BF)[:, :cap]

    def own_part(cols):
        block = tokens[:, cols]
        acc[:, cols] = dot(a_own, block)
        wide[:, cols] = dot(p_own, block)
    each_chunk(own_part)

    meta_in[d] = jnp.zeros(meta_in.shape[1:], F32)
    for k, j in enumerate(dps):
        arrival(meta_out.at[k], meta_in, meta_r, j).wait_recv()
    tri = upper[:LANES, :LANES]
    offset = kept
    seats, places = [], []
    for j in range(n_d):
        f = meta_in[j]
        placed, base = place(f[:slots], base, tri)
        valid = f[slots:slots + 1]
        seat = jnp.where(valid > 0, f[slots + 1:slots + 2] + offset, -1.0)
        offset = offset + jnp.sum(valid, axis=1, keepdims=True)
        a = (iota((BAL, LANES), 0) == seat).astype(F32)
        table = table + dot_nt(a, placed * f[:slots])
        seats.append(a.astype(BF)[:, :T_MAX])
        places.append(placed.astype(BF)[:, :first])

    rows_in[d] = jnp.zeros(rows_in.shape[1:], BF)
    for k, j in enumerate(dps):
        arrival(rows_out.at[k], rows_in, rows_r, j).wait_recv()
    send_rest(0, [partner] + near)

    def named_part(cols):
        total = wide[:, cols]
        for j in range(n_d):
            total = total + dot(places[j], rows_in[j, :, cols])
        wide[:, cols] = total
    each_chunk(named_part)

    def squares(c, carry):
        v = wide[:, pl.ds(pl.multiple_of(c * CHUNK, CHUNK), CHUNK)]
        return carry + jnp.sum(v * v, axis=1, keepdims=True)
    scale = lax.rsqrt(lax.fori_loop(0, chunks, squares, jnp.zeros((slots, 1), F32)) / width + EPSILON)

    def norm(cols):
        wide[:, cols] = wide[:, cols] * scale * gain[:, cols].astype(F32)
        for x in range(n_e):
            send1[x, :, cols] = wide[x * M:(x + 1) * M, cols].astype(BF)
    each_chunk(norm)

    one_copies = []
    for k, x in enumerate(exs):
        copy = remote(send1.at[x], recv1.at[e], s1.at[k], r1.at[e], {"expert": x})
        copy.start()
        one_copies.append(copy)
    recv1[e] = send1[e]
    for k, x in enumerate(exs):
        arrival(send1.at[x], recv1, r1, x, "expert").wait_recv()

    def gather(cols):
        for x in range(n_e):
            wide[x * M:(x + 1) * M, cols] = recv1[x, :, cols].astype(F32)
        recv2[d, :, cols] = wide[:, cols].astype(BF)
    each_chunk(gather)

    two_copies = []
    copy = remote(recv2.at[d], recv2.at[d], s2.at[0], r2.at[d], {"dp": partner})
    copy.start()
    two_copies.append(copy)
    for k, j in enumerate(near):
        copy = remote(recv2.at[d], recv2.at[d], s2.at[1 + k], r2.at[d], {"dp": j})
        copy.start()
        two_copies.append(copy)
    arrival(recv2.at[d], recv2, r2, partner).wait_recv()
    for k, j in enumerate(near):
        copy = remote(recv2.at[partner], recv2.at[partner], s2.at[half + k], r2.at[partner], {"dp": j})
        copy.start()
        two_copies.append(copy)

    def got_part(cols):
        total = acc[:, cols]
        for j in range(n_d):
            total = total + dot(seats[j][:, :first], rows_in[j, :, cols])
        acc[:, cols] = total
    each_chunk(got_part)
    for copy in loads:
        copy.wait()
    for j in near:
        arrival(recv2.at[d], recv2, r2, j).wait_recv()
        arrival(recv2.at[d], recv2, r2, lax.rem(j + half, n_d)).wait_recv()
    send_rest(0, across)

    gate[...] = jnp.zeros_like(gate)
    up[...] = jnp.zeros_like(up)

    def project(cols):
        x = recv2[:, :, cols].reshape(n_d * slots, CHUNK)
        gate[...] += dot(x, wg[cols, :])
        up[...] += dot(x, wu[cols, :])
    each_chunk(project)
    g = gate[...]
    hidden = (g / (1.0 + jnp.exp(-g)) * up[...]).astype(BF)
    for copy in two_copies:
        copy.wait_send()

    def down(cols):
        piece = dot(hidden, wd[:, cols]).astype(BF)
        recv2[:, :, cols] = piece.reshape(n_d, slots, CHUNK)
    each_chunk(down)
    three_copies = []
    for k, (j, p) in enumerate(zip(near, near_seats)):
        copy = remote(recv2.at[lax.rem(j + half, n_d)], part_in.at[seat_of],
                      sp.at[k], rp.at[seat_of], {"dp": j})
        copy.start()
        three_copies.append(copy)
    for k, (j, p) in enumerate(zip(near, near_seats)):
        copy = remote(recv2.at[j], recv3.at[seat_of], s3.at[k], r3.at[seat_of], {"dp": j})
        copy.start()
        three_copies.append(copy)
    send_rest(1, [partner])
    for p, j in zip(near_seats, near):
        remote(recv2.at[j], part_in.at[p], sp.at[0], rp.at[p], {"dp": j}).wait_recv()

    def partial_sum(cols):
        total = recv2[partner, :, cols].astype(F32)
        for p in near_seats:
            total = total + part_in[p, :, cols].astype(F32)
        part_out[:, cols] = total.astype(BF)
    each_chunk(partial_sum)
    copy = remote(part_out, recv3.at[half], s3.at[half - 1], r3.at[half], {"dp": partner})
    copy.start()
    three_copies.append(copy)
    send_rest(1, across + near)
    for p, j in zip(near_seats, near):
        remote(recv2.at[j], recv3.at[p], s3.at[0], r3.at[p], {"dp": j}).wait_recv()
    copy.wait_recv()

    def reduce(cols):
        total = recv2[d, :, cols].astype(F32) + recv3[half, :, cols].astype(F32)
        for p in near_seats:
            total = total + recv3[p, :, cols].astype(F32)
        wide[:, cols] = total
        for x in range(n_e):
            send4[x, :, cols] = wide[x * M:(x + 1) * M, cols].astype(BF)
    each_chunk(reduce)

    four_copies = []
    for k, x in enumerate(exs):
        copy = remote(send4.at[x], recv4.at[e], s4.at[k], r4.at[e], {"expert": x})
        copy.start()
        four_copies.append(copy)
    recv4[e] = send4[e]

    if rest:
        rest_in[d] = jnp.zeros(rest_in.shape[1:], BF)
        for b in range(rest // batch):
            for k, j in enumerate(dps):
                rest_copy(k, j, j, b).wait_recv()

        def rest_part(cols):
            total = acc[:, cols]
            for j in range(n_d):
                total = total + dot(seats[j][:, first:], rest_in[j, :, cols])
            acc[:, cols] = total
        each_chunk(rest_part)
    for k, x in enumerate(exs):
        arrival(send4.at[x], recv4, r4, x, "expert").wait_recv()
    table = table.astype(BF)

    def finish(cols):
        for x in range(n_e):
            wide[x * M:(x + 1) * M, cols] = recv4[x, :, cols].astype(F32)
        out[:, cols] = (acc[:, cols] + dot(table, wide[:, cols])).astype(BF)
    each_chunk(finish)
    for copy in meta_copies + row_copies + rest_copies + one_copies + three_copies + four_copies:
        copy.wait_send()


def body(tokens, counts, send_counts, routes, route_weights, norm_gain, w_gate, w_up, w_down):
    n_e, n_d = lax.axis_size("expert"), lax.axis_size("dp")
    cap, width = tokens.shape
    part = w_gate.shape[2]
    slots = n_e * M
    first = min(T_MAX, slots)
    rest = T_MAX - first
    height = slots + 8

    vmem = pl.BlockSpec(memory_space=pltpu.VMEM)
    smem = pl.BlockSpec(memory_space=pltpu.SMEM)
    hbm = pl.BlockSpec(memory_space=pl.ANY)
    dma = pltpu.SemaphoreType.DMA
    return pl.pallas_call(
        functools.partial(kernel, n_e, n_d),
        out_shape=jax.ShapeDtypeStruct((BAL, width), BF),
        in_specs=[smem] * 2 + [vmem] * 4 + [hbm] * 3,
        out_specs=vmem,
        scratch_shapes=[
            pltpu.VMEM((width, part), BF),
            pltpu.VMEM((width, part), BF),
            pltpu.VMEM((part, width), BF),
            pltpu.VMEM((n_d - 1, height, LANES), F32),
            pltpu.VMEM((n_d, height, LANES), F32),
            pltpu.VMEM((n_d - 1, first, width), BF),
            pltpu.VMEM((n_d - 1, max(rest, 16), width if rest else LANES), BF),
            pltpu.VMEM((n_d, first, width), BF),
            pltpu.VMEM((n_d, max(rest, 16), width if rest else LANES), BF),
            pltpu.VMEM((BAL, width), F32),
            pltpu.VMEM((slots, width), F32),
            pltpu.VMEM((n_e, M, width), BF),
            pltpu.VMEM((n_e, M, width), BF),
            pltpu.VMEM((n_d, slots, width), BF),
            pltpu.VMEM((n_d // 2 + 1, slots, width), BF),
            pltpu.VMEM((n_d // 2, slots, width), BF),
            pltpu.VMEM((slots, width), BF),
            pltpu.VMEM((n_e, M, width), BF),
            pltpu.VMEM((n_e, M, width), BF),
            pltpu.VMEM((n_d * slots, part), F32),
            pltpu.VMEM((n_d * slots, part), F32),
            dma((3,)),
            dma((n_d,)), dma((n_d,)),
            dma((n_d,)), dma((n_d,)),
            dma((2, n_d)), dma((2, n_d)),
            dma((n_e,)), dma((n_e,)),
            dma((n_d,)), dma((n_d,)),
            dma((n_d,)), dma((n_d,)),
            dma((n_d,)), dma((n_d,)),
            dma((n_e,)), dma((n_e,)),
        ],
        compiler_params=pltpu.CompilerParams(
            collective_id=0, has_side_effects=True, vmem_limit_bytes=60 * 1024 * 1024),
    )(counts, send_counts, tokens, routes, route_weights, norm_gain[None], w_gate[0], w_up[0], w_down[0])


def solution(mesh):
    rows = P(("group", "expert", "dp"), None)
    in_specs = (
        rows,
        P(("group", "expert", "dp")),
        rows,
        rows,
        rows,
        P(),
        P("expert", None, "dp"),
        P("expert", None, "dp"),
        P("expert", "dp", None),
    )
    return jax.shard_map(body, mesh=mesh, in_specs=in_specs, out_specs=rows, check_vma=False)
```

```python
import functools
import jax
import jax.numpy as jnp
from jax import lax
from jax.experimental import pallas as pl
from jax.experimental.pallas import tpu as pltpu
from jax.sharding import PartitionSpec as P

BAL = 96
T_MAX = 48
M = 4
EPSILON = 1e-06
LANES = 128
CHUNK = 3584
PARTS = 2
MESH = pl.DeviceIdType.MESH
BF = jnp.bfloat16
F32 = jnp.float32


def dot(a, b):
    return jnp.dot(a.astype(BF), b.astype(BF), preferred_element_type=F32)


def dot_nt(a, b):
    return lax.dot_general(
        a.astype(BF), b.astype(BF), (((1,), (1,)), ((), ())), preferred_element_type=F32
    )


def iota(shape, dim):
    return lax.broadcasted_iota(jnp.int32, shape, dim).astype(F32)


def kernel(n_e, n_d, counts, send_counts, tokens, routes, weights, gain, wg_hbm, wu_hbm, wd_hbm, out,
           wg, wu, wd, meta_out, meta_in, rows_out, rest_out, rows_in, rest_in,
           acc, wide, send1, recv1, recv2, recv3, part_in, part_out, send4, recv4, gate, up,
           w_sem, meta_s, meta_r, rows_s, rows_r, rest_s, rest_r,
           s1, r1, s2, r2, s3, r3, sp, rp, s4, r4):
    e, d = lax.axis_index("expert"), lax.axis_index("dp")
    width = tokens.shape[1]
    cap = tokens.shape[0]
    slots = n_e * M
    first = rows_out.shape[1]
    rest = T_MAX - first
    chunks = width // CHUNK
    dps = [lax.rem(d + k, n_d) for k in range(1, n_d)]
    exs = [lax.rem(e + k, n_e) for k in range(1, n_e)]
    half = n_d // 2
    seat_of = lax.rem(d, half)
    near_seats = [lax.rem(seat_of + k, half) for k in range(1, half)]
    near = [d - seat_of + p for p in near_seats]
    partner = lax.rem(d + half, n_d)

    per_part = chunks // PARTS
    parts = [pl.ds(q * (width // PARTS), width // PARTS) for q in range(PARTS)]

    def each_chunk(fn, q=None):
        def step(c, carry):
            fn(pl.ds(pl.multiple_of(c * CHUNK, CHUNK), CHUNK))
            return carry
        lo, hi = (0, chunks) if q is None else (q * per_part, (q + 1) * per_part)
        lax.fori_loop(lo, hi, step, 0)

    def remote(src, dst, send, recv, device):
        return pltpu.make_async_remote_copy(
            src_ref=src, dst_ref=dst, send_sem=send, recv_sem=recv,
            device_id=device, device_id_type=MESH)

    loads = [pltpu.make_async_copy(a, b, w_sem.at[i])
             for i, (a, b) in enumerate(((wg_hbm, wg), (wu_hbm, wu), (wd_hbm, wd)))]
    for copy in loads:
        copy.start()

    barrier = pltpu.get_barrier_semaphore()
    for j in dps:
        pl.semaphore_signal(barrier, inc=1, device_id={"dp": j}, device_id_type=MESH)
    for x in exs:
        pl.semaphore_signal(barrier, inc=1, device_id={"expert": x}, device_id_type=MESH)

    lanes = -(-cap // LANES) * LANES
    ids, values = routes[...], weights[...].astype(F32)
    wide_pad = jnp.zeros((1, lanes - cap), F32)
    picked = []
    for x in range(n_e):
        row = jnp.sum(jnp.where(ids == x, values, 0.0), axis=0, keepdims=True)
        picked.append(jnp.concatenate([row, wide_pad], axis=1))
    place_ids = lax.broadcasted_iota(jnp.int32, (1, lanes), 1)
    begin = counts[0]
    for j in range(n_d):
        begin = begin - send_counts[0, j]
    target = jnp.where(place_ids < begin, -1, -2)
    index = place_ids
    for j in range(n_d):
        after = begin + send_counts[0, j]
        inside = (place_ids >= begin) & (place_ids < after)
        target = jnp.where(inside, j, target)
        index = jnp.where(inside, place_ids - begin, index)
        begin = after
    target = target.astype(F32)
    valid = (target > -2.0).astype(F32)
    owner = lax.broadcasted_iota(jnp.int32, (slots, 1), 0) // M
    chosen = jnp.zeros((slots, lanes), F32)
    for x in range(n_e):
        chosen = jnp.where(owner == x, picked[x] * valid, chosen)
    named = (jnp.max(chosen, axis=0, keepdims=True) > 0).astype(F32)
    low = iota((8, lanes), 0)
    fields = jnp.concatenate([
        chosen, jnp.where(low == 0, valid, jnp.where(low == 1, index.astype(F32), 0.0))])
    upper = (iota((lanes, lanes), 0) < iota((lanes, lanes), 1)).astype(BF)
    picks = []
    for k, j in enumerate(dps):
        mine = (target == j.astype(F32)).astype(F32)
        ahead = mine * named
        behind = mine - ahead
        before_a = dot(jnp.broadcast_to(ahead, (8, lanes)), upper)[0:1]
        before_b = dot(jnp.broadcast_to(behind, (8, lanes)), upper)[0:1]
        total = jnp.sum(ahead, axis=1, keepdims=True)
        slot = jnp.where(ahead > 0, before_a, jnp.where(behind > 0, total + before_b, -1.0))
        pick = (iota((LANES, lanes), 0) == slot).astype(F32)
        meta_out[k] = dot_nt(fields, pick)
        picks.append(pick.astype(BF)[:T_MAX, :cap])

    pl.semaphore_wait(barrier, n_d - 1 + n_e - 1)
    meta_copies, row_copies, rest_copies = [], [], []
    for k, j in enumerate(dps):
        copy = remote(meta_out.at[k], meta_in.at[d], meta_s.at[k], meta_r.at[d], {"dp": j})
        copy.start()
        meta_copies.append(copy)
    head = jnp.concatenate([p[:first] for p in picks])

    def pack(cols):
        rows_out[:, :, cols] = dot(head, tokens[:, cols]).astype(BF).reshape(n_d - 1, first, CHUNK)
    each_chunk(pack)
    for k, j in enumerate(dps):
        copy = remote(rows_out.at[k], rows_in.at[d], rows_s.at[k], rows_r.at[d], {"dp": j})
        copy.start()
        row_copies.append(copy)
    if rest:
        tail = jnp.concatenate([p[first:] for p in picks])

        def pack_rest(cols):
            rest_out[:, :, cols] = dot(tail, tokens[:, cols]).astype(BF).reshape(n_d - 1, rest, CHUNK)
        each_chunk(pack_rest)
    batch = 16

    def rest_copy(k, j, slot, b):
        rows = pl.ds(b * batch, batch)
        return remote(rest_out.at[k, rows], rest_in.at[slot, rows],
                      rest_s.at[b, k], rest_r.at[b, slot], {"dp": j})

    across = [lax.rem(j + half, n_d) for j in near]

    def send_rest(b, peers):
        if b * batch < rest:
            for j in peers:
                k = lax.rem(j - d - 1 + 2 * n_d, n_d)
                copy = rest_copy(k, j, d, b)
                copy.start()
                rest_copies.append(copy)

    def arrival(src, buf, sems, j, axis="dp"):
        return remote(src, buf.at[j], sems.at[j], sems.at[j], {axis: j})

    own = (target == -1.0).astype(F32)
    kept = jnp.sum(own, axis=1, keepdims=True)
    own_f = fields * own
    rank_of = lax.broadcasted_iota(jnp.int32, (slots, 1), 0) % M
    rank_of = rank_of.astype(F32)
    base = jnp.zeros((slots, 1), F32)

    def place(weights, base, tri):
        has = (weights > 0).astype(F32)
        rank = dot(has, tri) + base
        placed = has * (rank == rank_of).astype(F32)
        return placed, base + jnp.sum(has, axis=1, keepdims=True)

    placed, base = place(own_f[:slots], base, upper)
    seat = jnp.where(own > 0, iota((1, lanes), 1), -1.0)
    a_own = (iota((BAL, lanes), 0) == seat).astype(F32)
    table = dot_nt(a_own, placed * own_f[:slots])
    a_own = a_own.astype(BF)[:, :cap]
    p_own = placed.astype(BF)[:, :cap]

    def own_part(cols):
        block = tokens[:, cols]
        acc[:, cols] = dot(a_own, block)
        wide[:, cols] = dot(p_own, block)
    each_chunk(own_part)

    meta_in[d] = jnp.zeros(meta_in.shape[1:], F32)
    for k, j in enumerate(dps):
        arrival(meta_out.at[k], meta_in, meta_r, j).wait_recv()
    tri = upper[:LANES, :LANES]
    offset = kept
    seats, places = [], []
    for j in range(n_d):
        f = meta_in[j]
        placed, base = place(f[:slots], base, tri)
        valid = f[slots:slots + 1]
        seat = jnp.where(valid > 0, f[slots + 1:slots + 2] + offset, -1.0)
        offset = offset + jnp.sum(valid, axis=1, keepdims=True)
        a = (iota((BAL, LANES), 0) == seat).astype(F32)
        table = table + dot_nt(a, placed * f[:slots])
        seats.append(a.astype(BF)[:, :T_MAX])
        places.append(placed.astype(BF)[:, :first])

    rows_in[d] = jnp.zeros(rows_in.shape[1:], BF)
    for k, j in enumerate(dps):
        arrival(rows_out.at[k], rows_in, rows_r, j).wait_recv()
    send_rest(0, [partner] + near)

    def named_part(cols):
        total = wide[:, cols]
        for j in range(n_d):
            total = total + dot(places[j], rows_in[j, :, cols])
        wide[:, cols] = total
    each_chunk(named_part)

    def squares(c, carry):
        v = wide[:, pl.ds(pl.multiple_of(c * CHUNK, CHUNK), CHUNK)]
        return carry + jnp.sum(v * v, axis=1, keepdims=True)
    scale = lax.rsqrt(lax.fori_loop(0, chunks, squares, jnp.zeros((slots, 1), F32)) / width + EPSILON)

    def norm(cols):
        wide[:, cols] = wide[:, cols] * scale * gain[cols].astype(F32).reshape(1, CHUNK)
        for x in range(n_e):
            send1[x, :, cols] = wide[x * M:(x + 1) * M, cols].astype(BF)
    one_copies = []
    for q, cols in enumerate(parts):
        each_chunk(norm, q)
        for k, x in enumerate(exs):
            copy = remote(send1.at[x, :, cols], recv1.at[e, :, cols],
                          s1.at[q, k], r1.at[q, e], {"expert": x})
            copy.start()
            one_copies.append(copy)
    recv1[e] = send1[e]

    def gather(cols):
        for x in range(n_e):
            wide[x * M:(x + 1) * M, cols] = recv1[x, :, cols].astype(F32)
        recv2[d, :, cols] = wide[:, cols].astype(BF)

    two_copies = []

    def block_copy(q, block, k, j):
        ref = recv2.at[block, :, parts[q]]
        return remote(ref, ref, s2.at[q, k], r2.at[q, block], {"dp": j})

    for q, cols in enumerate(parts):
        for k, x in enumerate(exs):
            remote(send1.at[x, :, cols], recv1.at[x, :, cols],
                   s1.at[q, k], r1.at[q, x], {"expert": x}).wait_recv()
        each_chunk(gather, q)
        for k, j in enumerate([partner] + near):
            copy = block_copy(q, d, k, j)
            copy.start()
            two_copies.append(copy)

    def got_part(cols):
        total = acc[:, cols]
        for j in range(n_d):
            total = total + dot(seats[j][:, :first], rows_in[j, :, cols])
        acc[:, cols] = total
    each_chunk(got_part)
    for copy in loads:
        copy.wait()
    gate[...] = jnp.zeros_like(gate)
    up[...] = jnp.zeros_like(up)

    def project(cols):
        x = recv2[:, :, cols].reshape(n_d * slots, CHUNK)
        gate[...] += dot(x, wg[cols, :])
        up[...] += dot(x, wu[cols, :])
    for q in range(PARTS):
        block_copy(q, partner, 0, partner).wait_recv()
        for k, j in enumerate(near):
            copy = block_copy(q, partner, half + k, j)
            copy.start()
            two_copies.append(copy)
    for q in range(PARTS):
        for j in near:
            block_copy(q, j, 0, j).wait_recv()
            block_copy(q, lax.rem(j + half, n_d), 0, j).wait_recv()
        if q == PARTS - 1:
            send_rest(0, across)
        each_chunk(project, q)
    g = gate[...]
    hidden = (g / (1.0 + jnp.exp(-g)) * up[...]).astype(BF)
    for copy in two_copies:
        copy.wait_send()

    def down(cols):
        piece = dot(hidden, wd[:, cols]).astype(BF)
        recv2[:, :, cols] = piece.reshape(n_d, slots, CHUNK)
    three_copies = []

    def part_copy(q, j, k, p):
        return remote(recv2.at[lax.rem(j + half, n_d), :, parts[q]], part_in.at[p, :, parts[q]],
                      sp.at[q, k], rp.at[q, p], {"dp": j})

    def near_copy(q, j, k, p):
        return remote(recv2.at[j, :, parts[q]], recv3.at[p, :, parts[q]],
                      s3.at[q, k], r3.at[q, p], {"dp": j})

    def far_copy(q):
        return remote(part_out.at[:, parts[q]], recv3.at[half, :, parts[q]],
                      s3.at[q, half - 1], r3.at[q, half], {"dp": partner})

    for q in range(PARTS):
        each_chunk(down, q)
        for k, j in enumerate(near):
            copy = part_copy(q, j, k, seat_of)
            copy.start()
            three_copies.append(copy)
    send_rest(1, [partner])

    def partial_sum(cols):
        total = recv2[partner, :, cols].astype(F32)
        for p in near_seats:
            total = total + part_in[p, :, cols].astype(F32)
        part_out[:, cols] = total.astype(BF)
    for q in range(PARTS):
        for p, j in zip(near_seats, near):
            part_copy(q, j, 0, p).wait_recv()
        each_chunk(partial_sum, q)
        copy = far_copy(q)
        copy.start()
        three_copies.append(copy)
        for k, j in enumerate(near):
            copy = near_copy(q, j, k, seat_of)
            copy.start()
            three_copies.append(copy)
    send_rest(1, across + near)

    def reduce(cols):
        total = recv2[d, :, cols].astype(F32) + recv3[half, :, cols].astype(F32)
        for p in near_seats:
            total = total + recv3[p, :, cols].astype(F32)
        wide[:, cols] = total
        for x in range(n_e):
            send4[x, :, cols] = wide[x * M:(x + 1) * M, cols].astype(BF)

    four_copies = []

    def back_copy(q, x, k, slot):
        return remote(send4.at[x, :, parts[q]], recv4.at[slot, :, parts[q]],
                      s4.at[q, k], r4.at[q, slot], {"expert": x})

    for q in range(PARTS):
        for p, j in zip(near_seats, near):
            near_copy(q, j, 0, p).wait_recv()
        far_copy(q).wait_recv()
        each_chunk(reduce, q)
        for k, x in enumerate(exs):
            copy = back_copy(q, x, k, e)
            copy.start()
            four_copies.append(copy)
    recv4[e] = send4[e]

    if rest:
        rest_in[d] = jnp.zeros(rest_in.shape[1:], BF)
        for b in range(rest // batch):
            for k, j in enumerate(dps):
                rest_copy(k, j, j, b).wait_recv()

        def rest_part(cols):
            total = acc[:, cols]
            for j in range(n_d):
                total = total + dot(seats[j][:, first:], rest_in[j, :, cols])
            acc[:, cols] = total
        each_chunk(rest_part)
    table = table.astype(BF)

    def finish(cols):
        for x in range(n_e):
            wide[x * M:(x + 1) * M, cols] = recv4[x, :, cols].astype(F32)
        out[:, cols] = (acc[:, cols] + dot(table, wide[:, cols])).astype(BF)
    for q in range(PARTS):
        for k, x in enumerate(exs):
            back_copy(q, x, k, x).wait_recv()
        each_chunk(finish, q)
    for copy in meta_copies + row_copies + rest_copies + one_copies + three_copies + four_copies:
        copy.wait_send()


def body(tokens, counts, send_counts, routes, route_weights, norm_gain, w_gate, w_up, w_down):
    n_e, n_d = lax.axis_size("expert"), lax.axis_size("dp")
    cap, width = tokens.shape
    part = w_gate.shape[2]
    slots = n_e * M
    first = min(T_MAX, slots)
    rest = T_MAX - first
    height = slots + 8

    vmem = pl.BlockSpec(memory_space=pltpu.VMEM)
    smem = pl.BlockSpec(memory_space=pltpu.SMEM)
    hbm = pl.BlockSpec(memory_space=pl.ANY)
    dma = pltpu.SemaphoreType.DMA
    return pl.pallas_call(
        functools.partial(kernel, n_e, n_d),
        out_shape=jax.ShapeDtypeStruct((BAL, width), BF),
        in_specs=[smem] * 2 + [vmem] * 4 + [hbm] * 3,
        out_specs=vmem,
        scratch_shapes=[
            pltpu.VMEM((width, part), BF),
            pltpu.VMEM((width, part), BF),
            pltpu.VMEM((part, width), BF),
            pltpu.VMEM((n_d - 1, height, LANES), F32),
            pltpu.VMEM((n_d, height, LANES), F32),
            pltpu.VMEM((n_d - 1, first, width), BF),
            pltpu.VMEM((n_d - 1, max(rest, 16), width if rest else LANES), BF),
            pltpu.VMEM((n_d, first, width), BF),
            pltpu.VMEM((n_d, max(rest, 16), width if rest else LANES), BF),
            pltpu.VMEM((BAL, width), F32),
            pltpu.VMEM((slots, width), F32),
            pltpu.VMEM((n_e, M, width), BF),
            pltpu.VMEM((n_e, M, width), BF),
            pltpu.VMEM((n_d, slots, width), BF),
            pltpu.VMEM((n_d // 2 + 1, slots, width), BF),
            pltpu.VMEM((n_d // 2, slots, width), BF),
            pltpu.VMEM((slots, width), BF),
            pltpu.VMEM((n_e, M, width), BF),
            pltpu.VMEM((n_e, M, width), BF),
            pltpu.VMEM((n_d * slots, part), F32),
            pltpu.VMEM((n_d * slots, part), F32),
            dma((3,)),
            dma((n_d,)), dma((n_d,)),
            dma((n_d,)), dma((n_d,)),
            dma((2, n_d)), dma((2, n_d)),
            dma((PARTS, n_e)), dma((PARTS, n_e)),
            dma((PARTS, n_d)), dma((PARTS, n_d)),
            dma((PARTS, n_d)), dma((PARTS, n_d)),
            dma((PARTS, n_d)), dma((PARTS, n_d)),
            dma((PARTS, n_e)), dma((PARTS, n_e)),
        ],
        compiler_params=pltpu.CompilerParams(
            collective_id=0, has_side_effects=True, vmem_limit_bytes=60 * 1024 * 1024),
    )(counts, send_counts, tokens, routes.T, route_weights.T, norm_gain, w_gate[0], w_up[0], w_down[0])


def solution(mesh):
    rows = P(("group", "expert", "dp"), None)
    in_specs = (
        rows,
        P(("group", "expert", "dp")),
        rows,
        rows,
        rows,
        P(),
        P("expert", None, "dp"),
        P("expert", None, "dp"),
        P("expert", "dp", None),
    )
    return jax.shard_map(body, mesh=mesh, in_specs=in_specs, out_specs=rows, check_vma=False)
```

```python
import functools
import jax
import jax.numpy as jnp
from jax import lax
from jax.experimental import pallas as pl
from jax.experimental.pallas import tpu as pltpu
from jax.sharding import PartitionSpec as P

BAL = 96
T_MAX = 48
M = 4
EPSILON = 1e-06
LANES = 128
CHUNK = 3584
PARTS = 2
MESH = pl.DeviceIdType.MESH
BF = jnp.bfloat16
F32 = jnp.float32


def dot(a, b):
    return jnp.dot(a.astype(BF), b.astype(BF), preferred_element_type=F32)


def dot_nt(a, b):
    return lax.dot_general(
        a.astype(BF), b.astype(BF), (((1,), (1,)), ((), ())), preferred_element_type=F32
    )


def iota(shape, dim):
    return lax.broadcasted_iota(jnp.int32, shape, dim).astype(F32)


def kernel(n_e, n_d, counts, send_counts, tokens, routes, weights, gain, wg_hbm, wu_hbm, wd_hbm, out,
           wg, wu, wd, meta_out, meta_in, rows_out, rest_out, rows_in, rest_in,
           acc, wide, send1, recv1, recv2, recv3, part_in, part_out, send4, recv4, gate, up,
           w_sem, meta_s, meta_r, rows_s, rows_r, rest_s, rest_r,
           s1, r1, s2, r2, s3, r3, sp, rp, s4, r4):
    e, d = lax.axis_index("expert"), lax.axis_index("dp")
    width = tokens.shape[1]
    cap = tokens.shape[0]
    slots = n_e * M
    first = rows_out.shape[1]
    rest = T_MAX - first
    chunks = width // CHUNK
    dps = [lax.rem(d + k, n_d) for k in range(1, n_d)]
    exs = [lax.rem(e + k, n_e) for k in range(1, n_e)]
    half = n_d // 2
    seat_of = lax.rem(d, half)
    near_seats = [lax.rem(seat_of + k, half) for k in range(1, half)]
    near = [d - seat_of + p for p in near_seats]
    partner = lax.rem(d + half, n_d)

    per_part = chunks // PARTS
    parts = [pl.ds(q * (width // PARTS), width // PARTS) for q in range(PARTS)]

    def each_chunk(fn, q=None):
        def step(c, carry):
            fn(pl.ds(pl.multiple_of(c * CHUNK, CHUNK), CHUNK))
            return carry
        lo, hi = (0, chunks) if q is None else (q * per_part, (q + 1) * per_part)
        lax.fori_loop(lo, hi, step, 0)

    def remote(src, dst, send, recv, device):
        return pltpu.make_async_remote_copy(
            src_ref=src, dst_ref=dst, send_sem=send, recv_sem=recv,
            device_id=device, device_id_type=MESH)

    loads = [pltpu.make_async_copy(a, b, w_sem.at[i])
             for i, (a, b) in enumerate(((wg_hbm, wg), (wu_hbm, wu), (wd_hbm, wd)))]
    for copy in loads:
        copy.start()

    barrier = pltpu.get_barrier_semaphore()
    for j in dps:
        pl.semaphore_signal(barrier, inc=1, device_id={"dp": j}, device_id_type=MESH)
    for x in exs:
        pl.semaphore_signal(barrier, inc=1, device_id={"expert": x}, device_id_type=MESH)

    lanes = -(-cap // LANES) * LANES
    ids, values = routes[...], weights[...].astype(F32)
    wide_pad = jnp.zeros((1, lanes - cap), F32)
    picked = []
    for x in range(n_e):
        row = jnp.sum(jnp.where(ids == x, values, 0.0), axis=0, keepdims=True)
        picked.append(jnp.concatenate([row, wide_pad], axis=1))
    place_ids = lax.broadcasted_iota(jnp.int32, (1, lanes), 1)
    begin = counts[0]
    for j in range(n_d):
        begin = begin - send_counts[0, j]
    target = jnp.where(place_ids < begin, -1, -2)
    index = place_ids
    for j in range(n_d):
        after = begin + send_counts[0, j]
        inside = (place_ids >= begin) & (place_ids < after)
        target = jnp.where(inside, j, target)
        index = jnp.where(inside, place_ids - begin, index)
        begin = after
    target = target.astype(F32)
    valid = (target > -2.0).astype(F32)
    owner = lax.broadcasted_iota(jnp.int32, (slots, 1), 0) // M
    chosen = jnp.zeros((slots, lanes), F32)
    for x in range(n_e):
        chosen = jnp.where(owner == x, picked[x] * valid, chosen)
    named = (jnp.max(chosen, axis=0, keepdims=True) > 0).astype(F32)
    low = iota((8, lanes), 0)
    fields = jnp.concatenate([
        chosen, jnp.where(low == 0, valid, jnp.where(low == 1, index.astype(F32), 0.0))])
    upper = (iota((lanes, lanes), 0) < iota((lanes, lanes), 1)).astype(BF)
    picks = []
    for k, j in enumerate(dps):
        mine = (target == j.astype(F32)).astype(F32)
        ahead = mine * named
        behind = mine - ahead
        before_a = dot(jnp.broadcast_to(ahead, (8, lanes)), upper)[0:1]
        before_b = dot(jnp.broadcast_to(behind, (8, lanes)), upper)[0:1]
        total = jnp.sum(ahead, axis=1, keepdims=True)
        slot = jnp.where(ahead > 0, before_a, jnp.where(behind > 0, total + before_b, -1.0))
        pick = (iota((LANES, lanes), 0) == slot).astype(F32)
        meta_out[k] = dot_nt(fields, pick)
        picks.append(pick.astype(BF)[:T_MAX, :cap])

    pl.semaphore_wait(barrier, n_d - 1 + n_e - 1)
    meta_copies, row_copies, rest_copies = [], [], []
    for k, j in enumerate(dps):
        copy = remote(meta_out.at[k], meta_in.at[d], meta_s.at[k], meta_r.at[d], {"dp": j})
        copy.start()
        meta_copies.append(copy)
    head = jnp.concatenate([p[:first] for p in picks])

    def pack(cols):
        rows_out[:, :, cols] = dot(head, tokens[:, cols]).astype(BF).reshape(n_d - 1, first, CHUNK)
    each_chunk(pack)
    across = [lax.rem(j + half, n_d) for j in near]
    for j in across + [partner] + near:
        k = lax.rem(j - d - 1 + 2 * n_d, n_d)
        copy = remote(rows_out.at[k], rows_in.at[d], rows_s.at[k], rows_r.at[d], {"dp": j})
        copy.start()
        row_copies.append(copy)
    if rest:
        tail = jnp.concatenate([p[first:] for p in picks])

        def pack_rest(cols):
            rest_out[:, :, cols] = dot(tail, tokens[:, cols]).astype(BF).reshape(n_d - 1, rest, CHUNK)
        each_chunk(pack_rest)
    batch = 16

    def rest_copy(k, j, slot, b):
        rows = pl.ds(b * batch, batch)
        return remote(rest_out.at[k, rows], rest_in.at[slot, rows],
                      rest_s.at[b, k], rest_r.at[b, slot], {"dp": j})

    def send_rest(b, peers):
        if b * batch < rest:
            for j in peers:
                k = lax.rem(j - d - 1 + 2 * n_d, n_d)
                copy = rest_copy(k, j, d, b)
                copy.start()
                rest_copies.append(copy)

    def arrival(src, buf, sems, j, axis="dp"):
        return remote(src, buf.at[j], sems.at[j], sems.at[j], {axis: j})

    own = (target == -1.0).astype(F32)
    kept = jnp.sum(own, axis=1, keepdims=True)
    own_f = fields * own
    rank_of = lax.broadcasted_iota(jnp.int32, (slots, 1), 0) % M
    rank_of = rank_of.astype(F32)
    base = jnp.zeros((slots, 1), F32)

    def place(weights, base, tri):
        has = (weights > 0).astype(F32)
        rank = dot(has, tri) + base
        placed = has * (rank == rank_of).astype(F32)
        return placed, base + jnp.sum(has, axis=1, keepdims=True)

    placed, base = place(own_f[:slots], base, upper)
    seat = jnp.where(own > 0, iota((1, lanes), 1), -1.0)
    a_own = (iota((BAL, lanes), 0) == seat).astype(F32)
    table = dot_nt(a_own, placed * own_f[:slots])
    a_own = a_own.astype(BF)[:, :cap]
    p_own = placed.astype(BF)[:, :cap]

    def own_part(cols):
        block = tokens[:, cols]
        acc[:, cols] = dot(a_own, block)
        wide[:, cols] = dot(p_own, block)
    each_chunk(own_part)

    meta_in[d] = jnp.zeros(meta_in.shape[1:], F32)
    for k, j in enumerate(dps):
        arrival(meta_out.at[k], meta_in, meta_r, j).wait_recv()
    tri = upper[:LANES, :LANES]
    offset = kept
    seats, places = [], []
    for j in range(n_d):
        f = meta_in[j]
        placed, base = place(f[:slots], base, tri)
        valid = f[slots:slots + 1]
        seat = jnp.where(valid > 0, f[slots + 1:slots + 2] + offset, -1.0)
        offset = offset + jnp.sum(valid, axis=1, keepdims=True)
        a = (iota((BAL, LANES), 0) == seat).astype(F32)
        table = table + dot_nt(a, placed * f[:slots])
        seats.append(a[:, :T_MAX])
        places.append(placed[:, :first])

    place_all = jnp.concatenate(places, axis=1).astype(BF)
    seat_head = jnp.concatenate([a[:, :first] for a in seats], axis=1).astype(BF)
    if rest:
        seat_tail = jnp.concatenate([a[:, first:] for a in seats], axis=1).astype(BF)
    rows_in[d] = jnp.zeros(rows_in.shape[1:], BF)
    for k, j in enumerate(dps):
        arrival(rows_out.at[k], rows_in, rows_r, j).wait_recv()
    send_rest(0, [partner] + near)

    def named_part(cols):
        block = rows_in[:, :, cols].reshape(n_d * first, CHUNK)
        wide[:, cols] += dot(place_all, block)
    each_chunk(named_part)

    def squares(c, carry):
        v = wide[:, pl.ds(pl.multiple_of(c * CHUNK, CHUNK), CHUNK)]
        return carry + jnp.sum(v * v, axis=1, keepdims=True)
    scale = lax.rsqrt(lax.fori_loop(0, chunks, squares, jnp.zeros((slots, 1), F32)) / width + EPSILON)

    def norm(cols):
        wide[:, cols] = wide[:, cols] * scale * gain[cols].astype(F32).reshape(1, CHUNK)
        for x in range(n_e):
            send1[x, :, cols] = wide[x * M:(x + 1) * M, cols].astype(BF)
    one_copies = []
    for q, cols in enumerate(parts):
        each_chunk(norm, q)
        for k, x in enumerate(exs):
            copy = remote(send1.at[x, :, cols], recv1.at[e, :, cols],
                          s1.at[q, k], r1.at[q, e], {"expert": x})
            copy.start()
            one_copies.append(copy)
    recv1[e] = send1[e]

    def gather(cols):
        for x in range(n_e):
            wide[x * M:(x + 1) * M, cols] = recv1[x, :, cols].astype(F32)
        recv2[d, :, cols] = wide[:, cols].astype(BF)

    two_copies = []

    def block_copy(q, block, k, j):
        ref = recv2.at[block, :, parts[q]]
        return remote(ref, ref, s2.at[q, k], r2.at[q, block], {"dp": j})

    for q, cols in enumerate(parts):
        for k, x in enumerate(exs):
            remote(send1.at[x, :, cols], recv1.at[x, :, cols],
                   s1.at[q, k], r1.at[q, x], {"expert": x}).wait_recv()
        each_chunk(gather, q)
        for k, j in enumerate([partner] + near):
            copy = block_copy(q, d, k, j)
            copy.start()
            two_copies.append(copy)

    def got_part(cols):
        block = rows_in[:, :, cols].reshape(n_d * first, CHUNK)
        acc[:, cols] += dot(seat_head, block)
    each_chunk(got_part)
    for copy in loads:
        copy.wait()
    gate[...] = jnp.zeros_like(gate)
    up[...] = jnp.zeros_like(up)

    def project(cols):
        x = recv2[:, :, cols].reshape(n_d * slots, CHUNK)
        gate[...] += dot(x, wg[cols, :])
        up[...] += dot(x, wu[cols, :])
    for q in range(PARTS):
        block_copy(q, partner, 0, partner).wait_recv()
        for k, j in enumerate(near):
            copy = block_copy(q, partner, half + k, j)
            copy.start()
            two_copies.append(copy)
    for q in range(PARTS):
        for j in near:
            block_copy(q, j, 0, j).wait_recv()
            block_copy(q, lax.rem(j + half, n_d), 0, j).wait_recv()
        if q == PARTS - 1:
            send_rest(0, across)
            send_rest(1, [partner])
        each_chunk(project, q)
    g = gate[...]
    hidden = (g / (1.0 + jnp.exp(-g)) * up[...]).astype(BF)
    for copy in two_copies:
        copy.wait_send()

    def down(cols):
        piece = dot(hidden, wd[:, cols]).astype(BF)
        recv2[:, :, cols] = piece.reshape(n_d, slots, CHUNK)
    three_copies = []

    def part_copy(q, j, k, p):
        return remote(recv2.at[lax.rem(j + half, n_d), :, parts[q]], part_in.at[p, :, parts[q]],
                      sp.at[q, k], rp.at[q, p], {"dp": j})

    def near_copy(q, j, k, p):
        return remote(recv2.at[j, :, parts[q]], recv3.at[p, :, parts[q]],
                      s3.at[q, k], r3.at[q, p], {"dp": j})

    def far_copy(q):
        return remote(part_out.at[:, parts[q]], recv3.at[half, :, parts[q]],
                      s3.at[q, half - 1], r3.at[q, half], {"dp": partner})

    for q in range(PARTS):
        each_chunk(down, q)
        for k, j in enumerate(near):
            copy = part_copy(q, j, k, seat_of)
            copy.start()
            three_copies.append(copy)

    def partial_sum(cols):
        total = recv2[partner, :, cols].astype(F32)
        for p in near_seats:
            total = total + part_in[p, :, cols].astype(F32)
        part_out[:, cols] = total.astype(BF)
    for q in range(PARTS):
        for p, j in zip(near_seats, near):
            part_copy(q, j, 0, p).wait_recv()
        each_chunk(partial_sum, q)
        copy = far_copy(q)
        copy.start()
        three_copies.append(copy)
        for k, j in enumerate(near):
            copy = near_copy(q, j, k, seat_of)
            copy.start()
            three_copies.append(copy)
    send_rest(1, across + near)

    def reduce(cols):
        total = recv2[d, :, cols].astype(F32) + recv3[half, :, cols].astype(F32)
        for p in near_seats:
            total = total + recv3[p, :, cols].astype(F32)
        wide[:, cols] = total
        for x in range(n_e):
            send4[x, :, cols] = wide[x * M:(x + 1) * M, cols].astype(BF)

    four_copies = []

    def back_copy(q, x, k, slot):
        return remote(send4.at[x, :, parts[q]], recv4.at[slot, :, parts[q]],
                      s4.at[q, k], r4.at[q, slot], {"expert": x})

    for q in range(PARTS):
        for p, j in zip(near_seats, near):
            near_copy(q, j, 0, p).wait_recv()
        far_copy(q).wait_recv()
        each_chunk(reduce, q)
        for k, x in enumerate(exs):
            copy = back_copy(q, x, k, e)
            copy.start()
            four_copies.append(copy)
    recv4[e] = send4[e]

    if rest:
        rest_in[d] = jnp.zeros(rest_in.shape[1:], BF)
        for b in range(rest // batch):
            for k, j in enumerate(dps):
                rest_copy(k, j, j, b).wait_recv()

        def rest_part(cols):
            block = rest_in[:, :, cols].reshape(n_d * rest, CHUNK)
            acc[:, cols] += dot(seat_tail, block)
        each_chunk(rest_part)
    table = table.astype(BF)

    def finish(cols):
        for x in range(n_e):
            wide[x * M:(x + 1) * M, cols] = recv4[x, :, cols].astype(F32)
        out[:, cols] = (acc[:, cols] + dot(table, wide[:, cols])).astype(BF)
    for q in range(PARTS):
        for k, x in enumerate(exs):
            back_copy(q, x, k, x).wait_recv()
        each_chunk(finish, q)
    for copy in meta_copies + row_copies + rest_copies + one_copies + three_copies + four_copies:
        copy.wait_send()


def body(tokens, counts, send_counts, routes, route_weights, norm_gain, w_gate, w_up, w_down):
    n_e, n_d = lax.axis_size("expert"), lax.axis_size("dp")
    cap, width = tokens.shape
    part = w_gate.shape[2]
    slots = n_e * M
    first = min(T_MAX, slots)
    rest = T_MAX - first
    height = slots + 8

    vmem = pl.BlockSpec(memory_space=pltpu.VMEM)
    smem = pl.BlockSpec(memory_space=pltpu.SMEM)
    hbm = pl.BlockSpec(memory_space=pl.ANY)
    dma = pltpu.SemaphoreType.DMA
    return pl.pallas_call(
        functools.partial(kernel, n_e, n_d),
        out_shape=jax.ShapeDtypeStruct((BAL, width), BF),
        in_specs=[smem] * 2 + [vmem] * 4 + [hbm] * 3,
        out_specs=vmem,
        scratch_shapes=[
            pltpu.VMEM((width, part), BF),
            pltpu.VMEM((width, part), BF),
            pltpu.VMEM((part, width), BF),
            pltpu.VMEM((n_d - 1, height, LANES), F32),
            pltpu.VMEM((n_d, height, LANES), F32),
            pltpu.VMEM((n_d - 1, first, width), BF),
            pltpu.VMEM((n_d - 1, max(rest, 16), width if rest else LANES), BF),
            pltpu.VMEM((n_d, first, width), BF),
            pltpu.VMEM((n_d, max(rest, 16), width if rest else LANES), BF),
            pltpu.VMEM((BAL, width), F32),
            pltpu.VMEM((slots, width), F32),
            pltpu.VMEM((n_e, M, width), BF),
            pltpu.VMEM((n_e, M, width), BF),
            pltpu.VMEM((n_d, slots, width), BF),
            pltpu.VMEM((n_d // 2 + 1, slots, width), BF),
            pltpu.VMEM((n_d // 2, slots, width), BF),
            pltpu.VMEM((slots, width), BF),
            pltpu.VMEM((n_e, M, width), BF),
            pltpu.VMEM((n_e, M, width), BF),
            pltpu.VMEM((n_d * slots, part), F32),
            pltpu.VMEM((n_d * slots, part), F32),
            dma((3,)),
            dma((n_d,)), dma((n_d,)),
            dma((n_d,)), dma((n_d,)),
            dma((2, n_d)), dma((2, n_d)),
            dma((PARTS, n_e)), dma((PARTS, n_e)),
            dma((PARTS, n_d)), dma((PARTS, n_d)),
            dma((PARTS, n_d)), dma((PARTS, n_d)),
            dma((PARTS, n_d)), dma((PARTS, n_d)),
            dma((PARTS, n_e)), dma((PARTS, n_e)),
        ],
        compiler_params=pltpu.CompilerParams(
            collective_id=0, has_side_effects=True, vmem_limit_bytes=60 * 1024 * 1024),
    )(counts, send_counts, tokens, routes.T, route_weights.T, norm_gain, w_gate[0], w_up[0], w_down[0])


def solution(mesh):
    rows = P(("group", "expert", "dp"), None)
    in_specs = (
        rows,
        P(("group", "expert", "dp")),
        rows,
        rows,
        rows,
        P(),
        P("expert", None, "dp"),
        P("expert", None, "dp"),
        P("expert", "dp", None),
    )
    return jax.shard_map(body, mesh=mesh, in_specs=in_specs, out_specs=rows, check_vma=False)
```
